512 devices in a mesh: dap: 64 (over y, x, z_hi), dp: 8 (over z_lo, core).
Axes of the slice: x: 4, y: 8, z: 8 (z_hi: 2, z_lo: 4; z = z_hi * 4 + z_lo), core: 2. Of those that a mesh axis runs over, the one named last changes fastest.
Arguments:
- homolog_tensor: bfloat16 [2048, 512, 256], P(('dp', 'dap')), parts along dimension 0, may hold values from -6 to 6
- couple_tensor: bfloat16 [4096, 512, 128], P(('dp', 'dap')), parts along dimension 0, may hold values from -6 to 6
- homolog_presence: int32 [2048, 512], P(('dp', 'dap')), parts along dimension 0, may hold values 0 or 1
- asking_matrix: bfloat16 [256, 256], replicated, may hold values from -0.71875 to 0.71875
- lookup_matrix: bfloat16 [256, 256], replicated, may hold values from -0.71875 to 0.71875
- content_matrix: bfloat16 [256, 256], replicated, may hold values from -0.375 to 0.375
- sigmoid_matrix: bfloat16 [256, 256], replicated, may hold values from -0.375 to 0.375
- sigmoid_offset: bfloat16 [256], replicated, may hold values from -4 to 4
- attention_final_matrix: bfloat16 [256, 256], replicated, may hold values from -0.75 to 0.75
- first_factor_matrix: bfloat16 [256, 32], replicated, may hold values from -0.375 to 0.375
- second_factor_matrix: bfloat16 [256, 32], replicated, may hold values from -0.375 to 0.375
- tensor_product_matrix: bfloat16 [1024, 128], replicated, may hold values from -3 to 3
- couple_offset_matrix: bfloat16 [128, 8], replicated, may hold values from -40 to 40
Outputs:
- homolog_revised: bfloat16 [2048, 512, 256], P(('dp', 'dap')), parts along dimension 0
- pair_updated: bfloat16 [4096, 512, 128], P(('dp', 'dap')), parts along dimension 0
The draws below stay inside these ranges and needn't reach their ends.
There are 8 independent parts, one for each index of `dp`. The reference program is written for one: setup_inputs(seed, part) draws one part's arguments, and reference() takes and returns one part's arrays. A program takes and returns all parts, laid end to end along the dimension named above; an argument that names none is the same for every part. Nothing has to cross between parts.
All inputs are finite; a program needn't handle non-finite values. No bound on the sum of `homolog_presence` on one device may be relied on, other than what follows from the above.
Results may differ from the reference program's by a relative error of at most 0.012.
The reference program's roundings to bfloat16 on the way count: a program that leaves them out, or rounds other values in their place, can miss the bound.
Values may be sent and summed in bfloat16 or wider, within the bound.
A program may use at most 128 MiB of HBM per device.

```python
import math
import jax
import jax.numpy as jnp
from jax import lax

ALIGNED_FEATURES = 256
CZ = 128
ATTENTION_HEADS = 8
PER_HEAD_WIDTH = 32
PROJECTED_WIDTH = 32
RES_DEV = 8
HOMOLOG_TOTAL = 256
CHAIN_LENGTH = 512
N_DAP = 64


def draw_couple_offset_matrix(key, part):
    key = jax.random.fold_in(key, 11)
    first, second = jax.random.split(key, 2)
    base = jnp.clip(jax.random.normal(first, (CZ, ATTENTION_HEADS), jnp.float32), -4.0, 4.0) / math.sqrt(CZ)
    factor = jnp.exp(jax.random.uniform(second, (1, ATTENTION_HEADS), jnp.float32, -0.2, 0.2))
    return jnp.clip(base * factor, -40.0, 40.0).astype(jnp.bfloat16)


def set_ends(result, key, smallest, high):
    spot = [jax.random.randint(jax.random.fold_in(key, axis), (), 0, length) for axis, length in enumerate(result.shape)]
    main_axis = result.shape.index(max(result.shape))
    beside = spot[:main_axis] + [(spot[main_axis] + 1) % result.shape[main_axis]] + spot[main_axis + 1:]
    return result.at[tuple(spot)].set(smallest).at[tuple(beside)].set(high)


def levels(stream_key, shape, cuts, smallest, largest):
    factor_of, own = 1.0, jax.random.fold_in(stream_key, 6)
    for dim, parts in cuts:
        steps = jnp.exp(jax.random.uniform(jax.random.fold_in(own, dim), (parts,), jnp.float32, smallest / len(cuts), largest / len(cuts)))
        factor_of = factor_of * jnp.repeat(steps, shape[dim] // parts).reshape([-1 if axis == dim else 1 for axis in range(len(shape))])
    return factor_of


def bell_draw(stream_key, dims, scale, limit, shards=(), kind=jnp.bfloat16):
    array = jax.random.normal(stream_key, dims, jnp.float32) * scale
    if len(shards) > 0:
        array = levels(stream_key, dims, shards, -0.22, 0.18) * array
    return jnp.clip(array, min=-limit, max=limit).astype(kind)


def setup_inputs(seed: int = 0, part: int = 0) -> dict:
    splits = jax.random.split(jax.random.key(seed), 14)
    part_splits = jax.random.split(jax.random.fold_in(splits[13], part), 14)
    return {
        "homolog_tensor": bell_draw(part_splits[0], (HOMOLOG_TOTAL, CHAIN_LENGTH, ALIGNED_FEATURES), 1.0, 6.0, ((0, 64),)),
        "couple_tensor": bell_draw(part_splits[1], (CHAIN_LENGTH, CHAIN_LENGTH, CZ), 1.0, 6.0, ((0, 64),)),
        "homolog_presence": set_ends((jax.random.randint(part_splits[2], (HOMOLOG_TOTAL, CHAIN_LENGTH), 0, 8) < 7).astype(jnp.int32), jax.random.fold_in(part_splits[2], 1), 0, 1),
        "asking_matrix": bell_draw(splits[3], (ALIGNED_FEATURES, ATTENTION_HEADS * PER_HEAD_WIDTH), 0.18, 0.71875),
        "lookup_matrix": bell_draw(splits[4], (ALIGNED_FEATURES, ATTENTION_HEADS * PER_HEAD_WIDTH), 0.18, 0.71875),
        "content_matrix": bell_draw(splits[5], (ALIGNED_FEATURES, ATTENTION_HEADS * PER_HEAD_WIDTH), ALIGNED_FEATURES ** -0.5, 0.375),
        "sigmoid_matrix": bell_draw(splits[6], (ALIGNED_FEATURES, ATTENTION_HEADS * PER_HEAD_WIDTH), ALIGNED_FEATURES ** -0.5, 0.375),
        "sigmoid_offset": bell_draw(splits[7], (ATTENTION_HEADS * PER_HEAD_WIDTH,), 1.0, 4.0),
        "attention_final_matrix": bell_draw(splits[8], (ATTENTION_HEADS * PER_HEAD_WIDTH, ALIGNED_FEATURES), (ATTENTION_HEADS * PER_HEAD_WIDTH // 4) ** -0.5, 0.75),
        "first_factor_matrix": bell_draw(splits[9], (ALIGNED_FEATURES, PROJECTED_WIDTH), ALIGNED_FEATURES ** -0.5, 0.375),
        "second_factor_matrix": bell_draw(splits[10], (ALIGNED_FEATURES, PROJECTED_WIDTH), ALIGNED_FEATURES ** -0.5, 0.375),
        "tensor_product_matrix": bell_draw(splits[11], (PROJECTED_WIDTH * PROJECTED_WIDTH, CZ), (max(PROJECTED_WIDTH * PROJECTED_WIDTH // HOMOLOG_TOTAL, 1)) ** -0.5, 3.0),
        "couple_offset_matrix": draw_couple_offset_matrix(jax.random.fold_in(splits[13], 71), part),
    }


def standardize_features(values):
    mean = lax.optimization_barrier(jnp.mean(values, axis=-1, keepdims=True))
    centered = values - mean
    variance = lax.optimization_barrier(jnp.mean(centered * centered, axis=-1, keepdims=True))
    return centered * lax.rsqrt(variance + 1e-05)

def reference(homolog_tensor, couple_tensor, homolog_presence, asking_matrix, lookup_matrix, content_matrix, sigmoid_matrix, sigmoid_offset, attention_final_matrix, first_factor_matrix, second_factor_matrix, tensor_product_matrix, couple_offset_matrix):
    sequence_mask = homolog_presence.astype(jnp.float32)
    standardized_lines = standardize_features(homolog_tensor.astype(jnp.float32)).astype(jnp.bfloat16)
    left_proj = (jnp.dot(standardized_lines, first_factor_matrix, preferred_element_type=jnp.float32) * sequence_mask[..., None]).astype(jnp.bfloat16)
    right_proj = (jnp.dot(standardized_lines, second_factor_matrix, preferred_element_type=jnp.float32) * sequence_mask[..., None]).astype(jnp.bfloat16)

    def opm_rows(start):
        left_rows = lax.dynamic_slice_in_dim(left_proj, start, RES_DEV, 1)
        mask_rows = lax.dynamic_slice_in_dim(sequence_mask, start, RES_DEV, 1)
        outer = jnp.einsum('sic,sjd->ijcd', left_rows.astype(jnp.float32), right_proj.astype(jnp.float32)).astype(jnp.bfloat16)
        projected = jnp.dot(outer.reshape(RES_DEV * CHAIN_LENGTH, PROJECTED_WIDTH * PROJECTED_WIDTH), tensor_product_matrix, preferred_element_type=jnp.float32)
        projected = projected.reshape(RES_DEV, CHAIN_LENGTH, CZ)
        counts = jnp.einsum('si,sj->ij', mask_rows, sequence_mask)
        return projected / (counts + 0.001)[..., None]
    starts = (jnp.arange(N_DAP) * RES_DEV).astype(jnp.int32)
    update = lax.map(opm_rows, starts).reshape(CHAIN_LENGTH, CHAIN_LENGTH, CZ)
    pair_updated = (couple_tensor.astype(jnp.float32) + update).astype(jnp.bfloat16)
    pair_normed = standardize_features(pair_updated.astype(jnp.float32))
    bias = jnp.einsum('ijc,ch->hij', pair_normed, couple_offset_matrix.astype(jnp.float32), precision=lax.Precision.HIGHEST)
    query = jnp.dot(standardized_lines, asking_matrix, preferred_element_type=jnp.float32).astype(jnp.bfloat16).reshape(HOMOLOG_TOTAL, CHAIN_LENGTH, ATTENTION_HEADS, PER_HEAD_WIDTH)
    key = jnp.dot(standardized_lines, lookup_matrix, preferred_element_type=jnp.float32).astype(jnp.bfloat16).reshape(HOMOLOG_TOTAL, CHAIN_LENGTH, ATTENTION_HEADS, PER_HEAD_WIDTH)
    value = jnp.dot(standardized_lines, content_matrix, preferred_element_type=jnp.float32).astype(jnp.bfloat16).reshape(HOMOLOG_TOTAL, CHAIN_LENGTH, ATTENTION_HEADS, PER_HEAD_WIDTH)
    gate = jax.nn.sigmoid(jnp.dot(standardized_lines, sigmoid_matrix, preferred_element_type=jnp.float32) + sigmoid_offset.astype(jnp.float32))
    key_mask = (sequence_mask - 1.0) * 10000.0
    scale = PER_HEAD_WIDTH ** (-0.5)

    def row_attention(items):
        query_seq, key_seq, value_seq, mask_seq = items
        scores = jnp.einsum('ihc,jhc->hij', query_seq.astype(jnp.float32), key_seq.astype(jnp.float32)) * scale
        scores = scores + bias + mask_seq[None, None, :]
        weights = jax.nn.softmax(scores, axis=-1).astype(jnp.bfloat16)
        attended = jnp.einsum('hij,jhc->ihc', weights.astype(jnp.float32), value_seq.astype(jnp.float32))
        return attended.reshape(CHAIN_LENGTH, ATTENTION_HEADS * PER_HEAD_WIDTH)
    attended = lax.map(row_attention, (query, key, value, key_mask))
    sigmoid_scaled_result = (attended * gate).astype(jnp.bfloat16)
    homolog_revised = (homolog_tensor.astype(jnp.float32) + jnp.dot(sigmoid_scaled_result, attention_final_matrix, preferred_element_type=jnp.float32)).astype(jnp.bfloat16)
    return (homolog_revised, pair_updated)
```

```python
import functools
import math

import jax
import jax.numpy as jnp
from jax import lax
from jax.experimental import pallas as pl
from jax.experimental.pallas import tpu as pltpu
from jax.sharding import PartitionSpec as P

MESH = pl.DeviceIdType.MESH
F32 = jnp.float32
BF16 = jnp.bfloat16
LOG2E = math.log2(math.e)
SCORE_SCALE = 32.0**-0.5 * LOG2E
PENALTY = (56576.0, -7.46875, 0.01123046875)

NY, NX, NZ = 8, 4, 2
PLANES = 36
ROWS = 48
YZ_OFFSETS = [(dy, dz) for dz in range(NZ) for dy in range(NY) if (dy, dz) != (0, 0)]
X_OFFSETS = (1, 3, 2)


def wrap(value, size):
    return lax.rem(value + size, size)


def index_of(y, x, z):
    return (y * NX + x) * NZ + z


def remote(src, dst, send, recv, device):
    return pltpu.make_async_remote_copy(
        src_ref=src,
        dst_ref=dst,
        send_sem=send,
        recv_sem=recv,
        device_id={"dap": device},
        device_id_type=MESH,
    )


class Ring:
    def __init__(self, where, whole, half, send, recv, zsend, zrecv):
        self.y, self.x, self.z = where
        self.whole, self.half = whole, half
        self.send, self.recv = send, recv
        self.zsend, self.zrecv = zsend, zrecv

    def plane(self, part):
        return self.z if part == 0 else 1 - self.z

    def copy(self, part, way, step, block):
        view = self.half(block, self.plane(part), way) if step == 3 else self.whole(block, self.plane(part))
        to = wrap(self.y + (1 if way == 0 else -1), NY)
        return remote(
            view,
            view,
            self.send.at[part, way, step],
            self.recv.at[part, way, step],
            index_of(to, self.x, self.z),
        )

    def send_block(self, part, way, step, block):
        self.copy(part, way, step, block).start()

    def partner(self, plane):
        view = self.whole(self.y, plane)
        return remote(view, view, self.zsend, self.zrecv, index_of(self.y, self.x, 1 - self.z))

    def start(self, part):
        if part == 1:
            self.partner(1 - self.z).wait_recv()
        for way in (0, 1):
            self.send_block(part, way, 0, self.y)

    def start_partner(self):
        self.partner(self.z).start()

    def step(self, part, number):
        for way in (0, 1):
            block = wrap(self.y + (-number if way == 0 else number), NY)
            self.copy(part, way, number - 1, block).wait_recv()
            self.send_block(part, way, number, block)

    def finish(self, part):
        for way in (0, 1):
            self.copy(part, way, 3, wrap(self.y + 4, NY)).wait_recv()

    def drain(self):
        self.partner(self.z).wait_send()
        for part in (0, 1):
            for way in (0, 1):
                for step in range(4):
                    self.copy(part, way, step, self.y).wait_send()


def perform(actions):
    for action in actions:
        action()


def normalize_rows(values):
    mean = jnp.mean(values, axis=-1, keepdims=True)
    centered = values - mean
    variance = jnp.mean(centered * centered, axis=-1, keepdims=True)
    return centered * lax.rsqrt(variance + 1e-05)


def nt_dot(left, right):
    return lax.dot_general(left, right, (((1,), (1,)), ((), ())), preferred_element_type=F32)


def kernel(
    hom,
    cpl,
    mask_rows,
    mask,
    mask_wide,
    w_proj,
    gate_offset,
    w_final,
    w_left,
    w_right_t,
    w_outer_t,
    w_bias_t,
    out_hom,
    out_pair,
    normed,
    l_send,
    l_all,
    r_send,
    r_got,
    r_wide,
    r_all,
    l_wide,
    l_mixed,
    l_t,
    qkv_send,
    qkv,
    gate,
    couple,
    counts,
    outer,
    pair_send,
    bias_block,
    bias,
    penalty,
    partial,
    att_send,
    att,
    x_send,
    x_recv,
    yz_send,
    yz_recv,
    ring_send,
    ring_recv,
    z_send,
    z_recv,
    own,
):
    me = lax.axis_index("dap")
    y = lax.div(me, NX * NZ)
    x = lax.rem(lax.div(me, NZ), NX)
    z = lax.rem(me, NZ)
    yz = y * NZ + z
    where = (y, x, z)

    barrier = pltpu.get_barrier_semaphore()
    for dx in X_OFFSETS:
        pl.semaphore_signal(
            barrier, inc=1, device_id={"dap": index_of(y, wrap(x + dx, NX), z)}, device_id_type=MESH
        )
    for dy, dz in YZ_OFFSETS:
        pl.semaphore_signal(
            barrier,
            inc=1,
            device_id={"dap": index_of(wrap(y + dy, NY), x, wrap(z + dz, NZ))},
            device_id_type=MESH,
        )

    lanes = lax.broadcasted_iota(jnp.int32, (512, 128), 1)

    def project(s, total):
        lines = normalize_rows(hom[s].astype(F32)).astype(BF16)
        normed[s] = lines
        left = jnp.dot(lines, w_left[...], preferred_element_type=F32)
        right = nt_dot(w_right_t[...], lines) * mask[pl.ds(s, 1), :]
        right = right.astype(BF16)
        for k in range(NX):
            r_send[k, s, 0:32, :] = right[:, 128 * k : 128 * k + 128]
            r_send[k, s, 32:48, :] = mask_rows[s]
        return jnp.where(lax.div(lanes, 32) == s, left, total)

    left = lax.fori_loop(0, 4, project, jnp.zeros((512, 128), F32))
    left = left * mask_wide[...]
    left = left.reshape(NY, NX, NZ, 8, 128)
    for b in range(NY):
        for c in range(NZ):
            l_send[b * NZ + c] = left[b, :, c].reshape(32, 128).astype(BF16)

    pl.semaphore_wait(barrier, len(X_OFFSETS) + len(YZ_OFFSETS))

    def over_x(kind, n, src, dst):
        to = index_of(y, wrap(x + X_OFFSETS[n], NX), z)
        return remote(src, dst, x_send.at[kind, n], x_recv.at[kind, n], to)

    def to_x(n):
        return wrap(x + X_OFFSETS[n], NX)

    def from_x(n):
        return wrap(x - X_OFFSETS[n], NX)

    sent = []

    def go(copy):
        copy.start()
        sent.append(copy)

    for n in range(3):
        go(over_x(0, n, r_send.at[to_x(n)], r_got.at[x]))
    for n, (dy, dz) in enumerate(YZ_OFFSETS):
        to_y, to_z = wrap(y + dy, NY), wrap(z + dz, NZ)
        go(
            remote(
                l_send.at[to_y * NZ + to_z],
                l_all.at[x, yz],
                yz_send.at[n],
                yz_recv.at[n],
                index_of(to_y, x, to_z),
            )
        )
    for n in range(3):
        go(over_x(1, n, cpl.at[:, pl.ds(pl.multiple_of(128 * to_x(n), 128), 128), :], couple.at[x]))
    own_copies = [
        pltpu.make_async_copy(r_send.at[x], r_got.at[x], own.at[0]),
        pltpu.make_async_copy(l_send.at[yz], l_all.at[x, yz], own.at[1]),
        pltpu.make_async_copy(
            cpl.at[:, pl.ds(pl.multiple_of(128 * x, 128), 128), :], couple.at[x], own.at[2]
        ),
    ]
    for copy in own_copies:
        copy.start()

    def heads(p, carry):
        for kind in range(4):
            w = w_proj[:, 256 * kind : 256 * kind + 256]
            first = jnp.dot(normed[2 * p], w, preferred_element_type=F32)
            second = jnp.dot(normed[2 * p + 1], w, preferred_element_type=F32)
            if kind == 3:
                first = jax.nn.sigmoid(first + gate_offset[...])
                second = jax.nn.sigmoid(second + gate_offset[...])
            for k in range(NX):
                both = jnp.concatenate(
                    [first[:, 64 * k : 64 * k + 64], second[:, 64 * k : 64 * k + 64]], axis=1
                )
                if kind == 3:
                    gate[k, p] = both
                else:
                    qkv_send[k, kind, p] = both.astype(BF16)
        return carry

    own_copies[0].wait()
    for n in range(3):
        over_x(0, n, r_send.at[0], r_got.at[from_x(n)]).wait_recv()
    r_wide[...] = r_got[...].astype(F32).reshape(16 * ROWS, 128)
    rows = pl.ds(pl.multiple_of(16 * yz, 16), 16)
    for q in range(PLANES):
        r_all[q, rows, :] = r_wide[pl.ds(q, 16, stride=ROWS), :].astype(BF16)

    def r_whole(b, c):
        return r_all.at[:, pl.ds(pl.multiple_of(16 * (b * NZ + c), 16), 16), :]

    def r_half(b, c, way):
        return r_all.at[
            pl.ds(way * (PLANES // 2), PLANES // 2),
            pl.ds(pl.multiple_of(16 * (b * NZ + c), 16), 16),
            :,
        ]

    ring = Ring(
        where, r_whole, r_half, ring_send.at[0], ring_recv.at[0], z_send.at[0], z_recv.at[0]
    )
    ring.start_partner()
    ring.start(0)

    own_copies[1].wait()
    for n, (dy, dz) in enumerate(YZ_OFFSETS):
        from_yz = wrap(y - dy, NY) * NZ + wrap(z - dz, NZ)
        remote(l_send.at[0], l_all.at[x, from_yz], yz_send.at[n], yz_recv.at[n], me).wait_recv()
    for n in range(3):
        go(over_x(2, n, l_all.at[x], l_all.at[x]))

    lax.fori_loop(0, 2, heads, 0)
    ring.step(0, 1)
    ring.start(1)
    for n in range(3):
        go(over_x(3, n, qkv_send.at[to_x(n)], qkv.at[x]))
    own_qkv = pltpu.make_async_copy(qkv_send.at[x], qkv.at[x], own.at[3])
    own_qkv.start()
    ring.step(0, 2)

    for n in range(3):
        over_x(2, n, l_all.at[x], l_all.at[from_x(n)]).wait_recv()
    l_wide[...] = l_all[...].astype(F32).reshape(2048, 128)
    for pair in range(16):
        block = jnp.concatenate(
            [l_wide[pl.ds(2 * pair, 64, stride=32), :], l_wide[pl.ds(2 * pair + 1, 64, stride=32), :]],
            axis=0,
        ).T
        for e in range(2):
            l_mixed[pl.ds((2 * pair + e) * 32, 32), :] = jnp.concatenate(
                [block[32 * s : 32 * s + 32, 64 * e : 64 * e + 64] for s in range(4)], axis=1
            ).astype(BF16)
    source = lax.broadcasted_iota(jnp.int32, (256, 256), 0)
    target = lax.broadcasted_iota(jnp.int32, (256, 256), 1)
    place = lax.rem(source, 16) * 16 + lax.rem(lax.div(source, 16), 4) * 4 + lax.div(source, 64)
    order = jnp.where(place == target, 1.0, 0.0).astype(BF16)
    l_t[...] = jnp.dot(l_mixed[...], order, preferred_element_type=F32).astype(BF16)

    ring.step(1, 1)
    ring.step(0, 3)
    ring.step(1, 2)
    ring.step(1, 3)
    ring.finish(0)
    ring.finish(1)

    plane = r_all[32 + lax.div(y, 2)].astype(F32).T.astype(BF16)
    together = jnp.dot(plane, r_all[32 + x], preferred_element_type=F32).astype(BF16)
    row = lax.broadcasted_iota(jnp.int32, (32, 128), 0)
    column = lax.broadcasted_iota(jnp.int32, (32, 128), 1)
    chosen = 64 * lax.rem(y, 2) + 16 * lax.div(row, 8) + 8 * z + lax.rem(row, 8)
    pick = jnp.where(chosen == column, 1.0, 0.0).astype(BF16)
    counts[...] = 1.0 / (jnp.dot(pick, together, preferred_element_type=F32) + 0.001)

    present = jnp.concatenate([r_all[32 + k, rows, :] for k in range(4)], axis=1).astype(F32) - 1.0
    penalty[...] = (
        jnp.concatenate(
            [present * PENALTY[0], present * PENALTY[1], present * PENALTY[2], jnp.zeros((80, 512), F32)],
            axis=0,
        )
        .T.astype(BF16)
    )

    own_copies[2].wait()
    for n in range(3):
        over_x(1, n, cpl.at[:, pl.ds(0, 128), :], couple.at[from_x(n)]).wait_recv()

    def outer_rows(g, carry):
        l_rows = l_t[pl.ds(pl.multiple_of(g * 256, 256), 256), :]
        for d in range(16):
            right = jnp.concatenate([r_all[2 * d], r_all[2 * d + 1]], axis=1)
            product = jnp.dot(l_rows, right, preferred_element_type=F32).astype(BF16)
            for e in range(2):
                outer[:, (2 * d + e) * 32 : (2 * d + e) * 32 + 32, :] = product[
                    :, 128 * e : 128 * e + 128
                ].reshape(8, 32, 128)
        offsets = []
        for pair in range(4):
            right = jnp.concatenate([outer[2 * pair], outer[2 * pair + 1]], axis=1)
            update = jnp.dot(w_outer_t[...], right, preferred_element_type=F32)
            for e in range(2):
                i = 2 * pair + e
                scaled = update[:, 128 * e : 128 * e + 128] * counts[pl.ds(g * 8 + i, 1), :]
                updated = (couple[g, i].astype(F32).T + scaled).astype(BF16).astype(F32)
                pair_send[g, i] = updated.T.astype(BF16)
                mean = jnp.mean(updated, axis=0, keepdims=True)
                centered = updated - mean
                variance = jnp.mean(centered * centered, axis=0, keepdims=True)
                standard = centered * lax.rsqrt(variance + 1e-05)
                offsets.append(
                    jnp.dot(
                        w_bias_t[...],
                        standard,
                        preferred_element_type=F32,
                        precision=lax.Precision.HIGHEST,
                    )
                    * LOG2E
                )
        for h in range(8):
            bias_block[h, g] = jnp.concatenate([v[h : h + 1] for v in offsets], axis=0)
        return carry

    lax.fori_loop(0, 4, outer_rows, 0)

    columns = pl.ds(pl.multiple_of(128 * x, 128), 128)
    for n in range(3):
        go(
            over_x(
                4,
                n,
                bias_block.at[pl.ds(2 * to_x(n), 2)],
                bias.at[:, y, :, z, :, columns],
            )
        )
    own_bias = pltpu.make_async_copy(
        bias_block.at[pl.ds(2 * x, 2)], bias.at[:, y, :, z, :, columns], own.at[4]
    )
    own_bias.start()
    own_bias.wait()
    for n in range(3):
        from_columns = pl.ds(pl.multiple_of(128 * from_x(n), 128), 128)
        over_x(
            4, n, bias_block.at[pl.ds(0, 2)], bias.at[:, y, :, z, :, from_columns]
        ).wait_recv()

    def bias_ring(h):
        def whole(b, c):
            return bias.at[h, b, :, c]

        def half(b, c, way):
            return bias.at[h, b, pl.ds(2 * way, 2), c]

        return Ring(
            where,
            whole,
            half,
            ring_send.at[1 + h],
            ring_recv.at[1 + h],
            z_send.at[1 + h],
            z_recv.at[1 + h],
        )

    low, high = bias_ring(0), bias_ring(1)
    low.start_partner()
    low.start(0)
    for n in range(3):
        go(over_x(5, n, pair_send.at[to_x(n)], out_pair.at[:, columns, :]))
    own_pair = pltpu.make_async_copy(pair_send.at[x], out_pair.at[:, columns, :], own.at[5])
    own_pair.start()
    low.step(0, 1)
    low.start(1)
    low.step(0, 2)
    low.step(1, 1)
    low.step(0, 3)
    low.step(1, 2)
    high.start_partner()
    high.start(0)
    low.step(1, 3)
    high.step(0, 1)
    low.finish(0)
    low.finish(1)

    groups = lax.div(lanes, 32)
    short_lanes = lax.broadcasted_iota(jnp.int32, (256, 128), 1)

    def attend(h, owner, p, first_pass):
        keys, values = [], []
        for e in range(2):
            inside = groups == 2 * e + h
            keys.append(
                jnp.concatenate(
                    [jnp.where(inside, qkv[owner, 1, p], jnp.zeros((), BF16)), penalty[...]], axis=1
                )
            )
            values.append(
                jnp.concatenate(
                    [
                        jnp.where(inside, qkv[owner, 2, p], jnp.zeros((), BF16)),
                        jnp.where(inside, 1.0, 0.0).astype(BF16),
                    ],
                    axis=1,
                )
            )
        values = jnp.concatenate(values, axis=0)
        for part in range(2):
            chunk = slice(256 * part, 256 * part + 256)
            offset = bias[h, 4 * part : 4 * part + 4].reshape(256, 512)
            weights = []
            for e in range(2):
                number = owner * 4 + 2 * p + e
                marked = (lax.rem(short_lanes, 16) == number) & (short_lanes < 48)
                query = jnp.concatenate(
                    [qkv[owner, 0, p, chunk, :], jnp.where(marked, 1.0, 0.0).astype(BF16)], axis=1
                )
                scores = nt_dot(query, keys[e]) * SCORE_SCALE + offset
                top = jnp.max(scores, axis=-1, keepdims=True)
                weights.append(jnp.exp2(scores - top).astype(BF16))
            both = jnp.dot(jnp.concatenate(weights, axis=1), values, preferred_element_type=F32)
            active = lax.rem(lax.div(short_lanes, 32), 2) == h
            result = jnp.where(active, both[:, :128] / both[:, 128:], 0.0)
            if first_pass:
                partial[owner, p, chunk, :] = result
            else:
                att_send[owner, p, chunk, :] = (partial[owner, p, chunk, :] + result).astype(BF16)

    def run(order, h, first_pass, before, after):
        def body(n, carry):
            for k, actions in before.items():
                pl.when(n == k)(functools.partial(perform, actions))
            slot = lax.div(n, 2)
            shift = jnp.int32(order[0])
            for k in range(1, 4):
                shift = jnp.where(slot == k, order[k], shift)
            attend(h, wrap(x + shift, NX), lax.rem(n, 2), first_pass)
            for k, actions in after.items():
                pl.when(n == k)(functools.partial(perform, actions))
            return carry

        lax.fori_loop(0, 8, body, 0)

    own_qkv.wait()

    def arrive(n):
        return lambda: over_x(3, n, qkv_send.at[0], qkv.at[from_x(n)]).wait_recv()

    run(
        (0, 3, 1, 2),
        0,
        True,
        {
            0: [lambda: high.start(1)],
            1: [lambda: high.step(0, 2)],
            2: [arrive(0), lambda: high.step(1, 1)],
            3: [lambda: high.step(0, 3)],
            4: [arrive(1), lambda: high.step(1, 2)],
            5: [lambda: high.step(1, 3)],
            6: [arrive(2)],
            7: [lambda: high.finish(0), lambda: high.finish(1)],
        },
        {},
    )

    def back(n):
        return lambda: over_x(6, n, att_send.at[to_x(n)], att.at[x]).start()

    run((2, 1, 3, 0), 1, False, {}, {1: [back(2)], 3: [back(0)], 5: [back(1)]})
    own_att = pltpu.make_async_copy(att_send.at[x], att.at[x], own.at[6])
    own_att.start()
    own_att.wait()
    for n in (2, 0, 1):
        over_x(6, n, att_send.at[0], att.at[from_x(n)]).wait_recv()

    nothing = jnp.zeros((64, 256), BF16)
    finals = []
    for e in range(2):
        parts = []
        for k in range(NX):
            piece = w_final[64 * k : 64 * k + 64, :]
            parts += [piece, nothing] if e == 0 else [nothing, piece]
        finals.append(jnp.concatenate(parts, axis=0))
    for p in range(2):
        gated = jnp.concatenate(
            [(att[k, p].astype(F32) * gate[k, p]).astype(BF16) for k in range(NX)], axis=1
        )
        for e in range(2):
            s = 2 * p + e
            out_hom[s] = (
                hom[s].astype(F32) + jnp.dot(gated, finals[e], preferred_element_type=F32)
            ).astype(BF16)

    own_pair.wait()
    for n in range(3):
        over_x(
            5,
            n,
            pair_send.at[0],
            out_pair.at[:, pl.ds(pl.multiple_of(128 * from_x(n), 128), 128), :],
        ).wait_recv()
    for n in range(3):
        over_x(6, n, att_send.at[to_x(n)], att.at[x]).wait_send()
    for copy in sent:
        copy.wait_send()
    for one in (ring, low, high):
        one.drain()


def on_device(
    homolog_tensor,
    couple_tensor,
    homolog_presence,
    asking_matrix,
    lookup_matrix,
    content_matrix,
    sigmoid_matrix,
    sigmoid_offset,
    attention_final_matrix,
    first_factor_matrix,
    second_factor_matrix,
    tensor_product_matrix,
    couple_offset_matrix,
):
    mask = homolog_presence.astype(F32)
    mask_rows = jnp.pad(
        homolog_presence.astype(BF16).reshape(4, 4, 128), ((0, 0), (0, 12), (0, 0))
    )
    mask_wide = jnp.repeat(mask.T, 32, axis=1)
    w_proj = jnp.concatenate([asking_matrix, lookup_matrix, content_matrix, sigmoid_matrix], axis=1)
    w_left = jnp.tile(first_factor_matrix, (1, 4))
    w_outer_t = tensor_product_matrix.reshape(32, 32, 128).transpose(2, 1, 0).reshape(128, 1024)
    vmem = pl.BlockSpec(memory_space=pltpu.VMEM)
    dma = pltpu.SemaphoreType.DMA
    scratch = [
        pltpu.VMEM((4, 512, 256), BF16),
        pltpu.VMEM((16, 32, 128), BF16),
        pltpu.VMEM((4, 16, 32, 128), BF16),
        pltpu.VMEM((4, 4, ROWS, 128), BF16),
        pltpu.VMEM((4, 4, ROWS, 128), BF16),
        pltpu.VMEM((16 * ROWS, 128), F32),
        pltpu.VMEM((PLANES, 256, 128), BF16),
        pltpu.VMEM((2048, 128), F32),
        pltpu.VMEM((1024, 256), BF16),
        pltpu.VMEM((1024, 256), BF16),
        pltpu.VMEM((4, 3, 2, 512, 128), BF16),
        pltpu.VMEM((4, 3, 2, 512, 128), BF16),
        pltpu.VMEM((4, 2, 512, 128), F32),
        pltpu.VMEM((4, 8, 128, 128), BF16),
        pltpu.VMEM((32, 128), F32),
        pltpu.VMEM((8, 1024, 128), BF16),
        pltpu.VMEM((4, 8, 128, 128), BF16),
        pltpu.VMEM((8, 4, 8, 128), F32),
        pltpu.VMEM((2, 8, 4, 2, 8, 512), F32),
        pltpu.VMEM((512, 128), BF16),
        pltpu.VMEM((4, 2, 512, 128), F32),
        pltpu.VMEM((4, 2, 512, 128), BF16),
        pltpu.VMEM((4, 2, 512, 128), BF16),
        dma((7, 3)),
        dma((7, 3)),
        dma((15,)),
        dma((15,)),
        dma((3, 2, 2, 4)),
        dma((3, 2, 2, 4)),
        dma((3,)),
        dma((3,)),
        dma((7,)),
    ]
    return pl.pallas_call(
        kernel,
        name="evoformer_block",
        out_shape=(
            jax.ShapeDtypeStruct((4, 512, 256), BF16),
            jax.ShapeDtypeStruct((8, 512, 128), BF16),
        ),
        in_specs=[vmem] * 12,
        out_specs=(vmem, vmem),
        scratch_shapes=scratch,
        compiler_params=pltpu.CompilerParams(
            collective_id=1, has_side_effects=True, vmem_limit_bytes=60 << 20
        ),
    )(
        homolog_tensor,
        couple_tensor,
        mask_rows,
        mask,
        mask_wide,
        w_proj,
        sigmoid_offset.astype(F32).reshape(1, 256),
        attention_final_matrix,
        w_left,
        second_factor_matrix.T,
        w_outer_t,
        couple_offset_matrix.T.astype(F32),
    )


def solution(mesh):
    return jax.shard_map(
        on_device,
        mesh=mesh,
        in_specs=(
            P(("dp", "dap"), None, None),
            P(("dp", "dap"), None, None),
            P(("dp", "dap"), None),
            P(),
            P(),
            P(),
            P(),
            P(),
            P(),
            P(),
            P(),
            P(),
            P(),
        ),
        out_specs=(P(("dp", "dap"), None, None), P(("dp", "dap"), None, None)),
        check_vma=False,
    )
```

```python
import functools
import math

import jax
import jax.numpy as jnp
from jax import lax
from jax.experimental import pallas as pl
from jax.experimental.pallas import tpu as pltpu
from jax.sharding import PartitionSpec as P

MESH = pl.DeviceIdType.MESH
F32 = jnp.float32
BF16 = jnp.bfloat16
LOG2E = math.log2(math.e)
SCORE_SCALE = 32.0**-0.5 * LOG2E
PENALTY = (56576.0, -7.46875, 0.01123046875)

NY, NX, NZ = 8, 4, 2
PLANES = 36
ROWS = 48
YZ_OFFSETS = [(dy, dz) for dz in range(NZ) for dy in range(NY) if (dy, dz) != (0, 0)]
X_OFFSETS = (1, 3, 2)
XZ_OFFSETS = [(dx, dz) for dx in (1, 3, 2, 0) for dz in range(NZ) if (dx, dz) != (0, 0)]


def wrap(value, size):
    return lax.rem(value + size, size)


def index_of(y, x, z):
    return (y * NX + x) * NZ + z


def remote(src, dst, send, recv, device):
    return pltpu.make_async_remote_copy(
        src_ref=src,
        dst_ref=dst,
        send_sem=send,
        recv_sem=recv,
        device_id={"dap": device},
        device_id_type=MESH,
    )


class Ring:
    def __init__(self, where, whole, half, send, recv):
        self.y, self.x, self.z = where
        self.whole, self.half = whole, half
        self.send, self.recv = send, recv

    def copy(self, way, step, block):
        view = self.half(block, way) if step == 3 else self.whole(block)
        to = wrap(self.y + (1 if way == 0 else -1), NY)
        return remote(
            view, view, self.send.at[way, step], self.recv.at[way, step], index_of(to, self.x, self.z)
        )

    def start(self):
        for way in (0, 1):
            self.copy(way, 0, self.y).start()

    def step(self, number):
        for way in (0, 1):
            block = wrap(self.y + (-number if way == 0 else number), NY)
            self.copy(way, number - 1, block).wait_recv()
            self.copy(way, number, block).start()

    def finish(self):
        for way in (0, 1):
            self.copy(way, 3, wrap(self.y + 4, NY)).wait_recv()

    def drain(self):
        for way in (0, 1):
            for step in range(4):
                self.copy(way, step, self.y).wait_send()


def regroup(v0, v1, v2, v3):
    lane = lax.broadcasted_iota(jnp.int32, v0.shape, 1)
    low = lane < 64
    even = lax.rem(lax.div(lane, 32), 2) == 0
    u0 = jnp.where(low, v0, pltpu.roll(v2, 64, 1))
    u2 = jnp.where(low, pltpu.roll(v0, 64, 1), v2)
    u1 = jnp.where(low, v1, pltpu.roll(v3, 64, 1))
    u3 = jnp.where(low, pltpu.roll(v1, 64, 1), v3)
    return (
        jnp.where(even, u0, pltpu.roll(u1, 32, 1)),
        jnp.where(even, pltpu.roll(u0, 96, 1), u1),
        jnp.where(even, u2, pltpu.roll(u3, 32, 1)),
        jnp.where(even, pltpu.roll(u2, 96, 1), u3),
    )


def perform(actions):
    for action in actions:
        action()


def normalize_rows(values):
    mean = jnp.mean(values, axis=-1, keepdims=True)
    centered = values - mean
    variance = jnp.mean(centered * centered, axis=-1, keepdims=True)
    return centered * lax.rsqrt(variance + 1e-05)


def nt_dot(left, right):
    return lax.dot_general(left, right, (((1,), (1,)), ((), ())), preferred_element_type=F32)


def kernel(
    hom,
    cpl,
    presence,
    w_query,
    w_key,
    w_value,
    w_gate,
    gate_offset,
    w_left_t,
    w_right_t,
    w_outer,
    w_bias_t,
    out_gated,
    out_pair,
    normed,
    l_send,
    l_all,
    r_send,
    r_got,
    r_wide,
    r_all,
    l_wide,
    l_mixed,
    l_t,
    w_outer_wide,
    w_outer_t,
    qv_send,
    qv,
    k_send,
    k_got,
    gate,
    couple,
    couple_t,
    updated_t,
    counts,
    outer,
    pair_send,
    bias_block,
    bias,
    penalty,
    att_send,
    att,
    x_send,
    x_recv,
    xz_send,
    xz_recv,
    yz_send,
    yz_recv,
    ring_send,
    ring_recv,
    own,
):
    me = lax.axis_index("dap")
    y = lax.div(me, NX * NZ)
    x = lax.rem(lax.div(me, NZ), NX)
    z = lax.rem(me, NZ)
    yz = y * NZ + z
    where = (y, x, z)

    barrier = pltpu.get_barrier_semaphore()
    for dx, dz in XZ_OFFSETS:
        if dx != 0:
            pl.semaphore_signal(
                barrier,
                inc=1,
                device_id={"dap": index_of(y, wrap(x + dx, NX), wrap(z + dz, NZ))},
                device_id_type=MESH,
            )
    for dy, dz in YZ_OFFSETS:
        pl.semaphore_signal(
            barrier,
            inc=1,
            device_id={"dap": index_of(wrap(y + dy, NY), x, wrap(z + dz, NZ))},
            device_id_type=MESH,
        )

    def over_x(kind, n, src, dst):
        to = index_of(y, wrap(x + X_OFFSETS[n], NX), z)
        return remote(src, dst, x_send.at[kind, n], x_recv.at[kind, n], to)

    def over_xz(kind, n, src, dst):
        dx, dz = XZ_OFFSETS[n]
        to = index_of(y, wrap(x + dx, NX), wrap(z + dz, NZ))
        return remote(src, dst, xz_send.at[kind, n], xz_recv.at[kind, n], to)

    def to_xz(n):
        return wrap(x + XZ_OFFSETS[n][0], NX)

    def from_xz(n):
        dx, dz = XZ_OFFSETS[n]
        return wrap(x - dx, NX), wrap(z - dz, NZ)

    def to_x(n):
        return wrap(x + X_OFFSETS[n], NX)

    def from_x(n):
        return wrap(x - X_OFFSETS[n], NX)

    sent = []

    def go(copy):
        copy.start()
        sent.append(copy)

    def block_of(k):
        return pl.ds(pl.multiple_of(128 * k, 128), 128)

    lanes = lax.broadcasted_iota(jnp.int32, (512, 128), 1)
    groups = lax.div(lanes, 32)
    w_left = jnp.concatenate([w_left_t[...]] * 4, axis=0)

    def project(s, total):
        lines = normalize_rows(hom[s].astype(F32)).astype(BF16)
        normed[s] = lines
        left = nt_dot(lines, w_left)
        present = presence[pl.ds(s, 1), :].astype(F32)
        right = (nt_dot(w_right_t[...], lines) * present).astype(BF16)
        rows = jnp.concatenate(
            [present[:, 128 * k : 128 * k + 128] for k in range(4)] + [jnp.zeros((12, 128), F32)], axis=0
        ).astype(BF16)
        for k in range(NX):
            r_send[k, s, 0:32, :] = right[:, 128 * k : 128 * k + 128]
            r_send[k, s, 32:48, :] = rows
        return jnp.where(groups == s, left, total)

    left = lax.fori_loop(0, 4, project, jnp.zeros((512, 128), F32))
    spread = jnp.where(
        lax.div(lax.broadcasted_iota(jnp.int32, (128, 128), 1), 32)
        == lax.broadcasted_iota(jnp.int32, (128, 128), 0),
        1.0,
        0.0,
    ).astype(BF16)
    tall = jnp.concatenate([presence[...].astype(F32), jnp.zeros((124, 512), F32)], axis=0).T
    left = left * jnp.dot(tall.astype(BF16), spread, preferred_element_type=F32)
    left = left.reshape(NY, NX, NZ, 8, 128)
    for b in range(NY):
        for c in range(NZ):
            l_send[b * NZ + c] = left[b, :, c].reshape(32, 128).astype(BF16)

    pl.semaphore_wait(barrier, 6 + len(YZ_OFFSETS))

    for n in range(7):
        go(over_xz(0, n, r_send.at[to_xz(n)], r_got.at[z, x]))
    for n, (dy, dz) in enumerate(YZ_OFFSETS):
        to_y, to_z = wrap(y + dy, NY), wrap(z + dz, NZ)
        go(
            remote(
                l_send.at[to_y * NZ + to_z],
                l_all.at[x, yz],
                yz_send.at[n],
                yz_recv.at[n],
                index_of(to_y, x, to_z),
            )
        )
    for n in range(3):
        go(over_x(1, n, cpl.at[:, block_of(to_x(n)), :], couple.at[x]))
    own_copies = [
        pltpu.make_async_copy(r_send.at[x], r_got.at[z, x], own.at[0]),
        pltpu.make_async_copy(l_send.at[yz], l_all.at[x, yz], own.at[1]),
        pltpu.make_async_copy(cpl.at[:, block_of(x), :], couple.at[x], own.at[2]),
    ]
    for copy in own_copies:
        copy.start()

    def heads(part, carry):
        rows = pl.ds(pl.multiple_of(128 * part, 128), 128)
        for kind, w in enumerate((w_query, w_value, w_gate)):
            made = [jnp.dot(normed[s, rows, :], w[...], preferred_element_type=F32) for s in range(4)]
            if kind == 2:
                made = [jax.nn.sigmoid(m + gate_offset[...]) for m in made]
            for b in range(2):
                outs = regroup(*[m[:, 128 * b : 128 * b + 128] for m in made])
                for t in range(4):
                    h = 4 * b + t
                    if kind == 2:
                        gate[h // 2, h % 2, rows, :] = outs[t]
                    else:
                        qv_send[h // 2, h % 2, kind, pl.ds(2 * part, 2)] = (
                            outs[t].astype(BF16).reshape(2, 4, 16, 128)
                        )
        return carry

    w_key_t = w_key[...].astype(F32).T.astype(BF16)

    def keys(s, carry):
        made = nt_dot(w_key_t, normed[s]).astype(BF16)
        for h in range(8):
            k_send[h // 2, h % 2, pl.ds(pl.multiple_of(32 * s, 32), 32), :] = made[32 * h : 32 * h + 32]
        return carry

    lax.fori_loop(0, 4, keys, 0)
    lax.fori_loop(0, 4, heads, 0)

    def qkv_copies(h, n):
        other = from_x(n)
        return (
            (5 + 3 * h, k_send.at[to_x(n), h], k_got.at[x, h], k_got.at[other, h]),
            (6 + 3 * h, qv_send.at[to_x(n), h, 1], qv.at[x, h, 1], qv.at[other, h, 1]),
            (7 + 3 * h, qv_send.at[to_x(n), h, 0], qv.at[x, h, 0], qv.at[other, h, 0]),
        )

    def send_qkv(h, kinds=(0, 1, 2)):
        for k in kinds:
            for n in range(3):
                kind, src, dst, _ = qkv_copies(h, n)[k]
                go(over_x(kind, n, src, dst))

    def arrive_qkv(h, n):
        for kind, src, _, got in qkv_copies(h, n):
            over_x(kind, n, src, got).wait_recv()

    own_qkv = [
        pltpu.make_async_copy(k_send.at[x], k_got.at[x], own.at[3]),
        pltpu.make_async_copy(qv_send.at[x], qv.at[x], own.at[7]),
    ]
    for copy in own_qkv:
        copy.start()

    own_copies[0].wait()
    for n in range(7):
        other_x, other_z = from_xz(n)
        over_xz(0, n, r_send.at[0], r_got.at[other_z, other_x]).wait_recv()
    r_wide[...] = r_got[...].astype(F32).reshape(32 * ROWS, 128)

    def line_of(b):
        return pl.ds(pl.multiple_of(32 * b, 32), 32)

    for q in range(PLANES):
        r_all[q, line_of(y), :] = r_wide[pl.ds(q, 32, stride=ROWS), :].astype(BF16)

    def right_ring(c):
        first = (0, 18)[c]

        def whole(b):
            return r_all.at[pl.ds(first, 18), line_of(b), :]

        def half(b, way):
            return r_all.at[pl.ds(first + 9 * way, 9), line_of(b), :]

        return Ring(where, whole, half, ring_send.at[c], ring_recv.at[c])

    near, rest = right_ring(0), right_ring(1)
    near.start()
    rest.start()

    own_copies[1].wait()
    for n, (dy, dz) in enumerate(YZ_OFFSETS):
        from_yz = wrap(y - dy, NY) * NZ + wrap(z - dz, NZ)
        remote(l_send.at[0], l_all.at[x, from_yz], yz_send.at[n], yz_recv.at[n], me).wait_recv()
    for n in range(3):
        go(over_x(0, n, l_all.at[x], l_all.at[x]))
    send_qkv(0)

    w_outer_wide[...] = w_outer[...].astype(F32)
    for k in range(8):
        w_outer_t[:, 128 * k : 128 * k + 128] = (
            jnp.concatenate([w_outer_wide[pl.ds(4 * k + t, 32, stride=32), :] for t in range(4)], axis=0)
            .T.astype(BF16)
        )

    near.step(1)
    rest.step(1)

    for n in range(3):
        over_x(0, n, l_all.at[x], l_all.at[from_x(n)]).wait_recv()
    l_wide[...] = l_all[...].astype(F32).reshape(2048, 128)
    for pair in range(16):
        block = jnp.concatenate(
            [l_wide[pl.ds(2 * pair, 64, stride=32), :], l_wide[pl.ds(2 * pair + 1, 64, stride=32), :]],
            axis=0,
        ).T
        for e in range(2):
            l_mixed[pl.ds((2 * pair + e) * 32, 32), :] = jnp.concatenate(
                [block[32 * s : 32 * s + 32, 64 * e : 64 * e + 64] for s in range(4)], axis=1
            ).astype(BF16)
    source = lax.broadcasted_iota(jnp.int32, (256, 256), 0)
    target = lax.broadcasted_iota(jnp.int32, (256, 256), 1)
    place = lax.rem(source, 16) * 16 + lax.rem(lax.div(source, 16), 4) * 4 + lax.div(source, 64)
    order = jnp.where(place == target, 1.0, 0.0).astype(BF16)
    l_t[...] = jnp.dot(l_mixed[...], order, preferred_element_type=F32).astype(BF16)

    near.step(2)
    rest.step(2)

    own_copies[2].wait()
    for n in range(3):
        over_x(1, n, cpl.at[:, pl.ds(0, 128), :], couple.at[from_x(n)]).wait_recv()

    def turn_couple(g, carry):
        for i in range(8):
            couple_t[g, i] = couple[g, i].astype(F32).T
        return carry

    lax.fori_loop(0, 4, turn_couple, 0)
    near.step(3)
    send_qkv(1, (0, 1))
    rest.step(3)
    near.finish()

    def outer_rows(g, first, last):
        l_rows = l_t[pl.ds(pl.multiple_of(g * 256, 256), 256), :]
        for d in range(first, last):
            right = jnp.concatenate([r_all[2 * d], r_all[2 * d + 1]], axis=1)
            product = jnp.dot(l_rows, right, preferred_element_type=F32).astype(BF16)
            for e in range(2):
                outer[pl.ds(8 * g, 8), (2 * d + e) * 32 : (2 * d + e) * 32 + 32, :] = product[
                    :, 128 * e : 128 * e + 128
                ].reshape(8, 32, 128)

    def outer_near(g, carry):
        outer_rows(g, 0, 9)
        return carry

    lax.fori_loop(0, 4, outer_near, 0)
    rest.finish()

    plane = r_all[32 + lax.div(y, 2)].astype(F32).T.astype(BF16)
    together = jnp.dot(plane, r_all[32 + x], preferred_element_type=F32).astype(BF16)
    row = lax.broadcasted_iota(jnp.int32, (32, 128), 0)
    column = lax.broadcasted_iota(jnp.int32, (32, 128), 1)
    chosen = 64 * lax.rem(y, 2) + 16 * lax.div(row, 8) + 8 * z + lax.rem(row, 8)
    pick = jnp.where(chosen == column, 1.0, 0.0).astype(BF16)
    counts[...] = 1.0 / (jnp.dot(pick, together, preferred_element_type=F32) + 0.001)

    w_bias = jnp.concatenate([w_bias_t[...]] * 3, axis=1)

    def outer_rest(g, carry):
        outer_rows(g, 9, 16)
        offsets = []
        for pair in range(4):
            right = jnp.concatenate([outer[8 * g + 2 * pair], outer[8 * g + 2 * pair + 1]], axis=1)
            update = jnp.dot(w_outer_t[...], right, preferred_element_type=F32)
            standards = []
            for e in range(2):
                i = 2 * pair + e
                scaled = update[:, 128 * e : 128 * e + 128] * counts[pl.ds(g * 8 + i, 1), :]
                updated = (couple_t[g, i] + scaled).astype(BF16)
                updated_t[g, i] = updated
                updated = updated.astype(F32)
                mean = jnp.mean(updated, axis=0, keepdims=True)
                centered = updated - mean
                variance = jnp.mean(centered * centered, axis=0, keepdims=True)
                standards.append(centered * lax.rsqrt(variance + 1e-05))
            standard = jnp.concatenate(standards, axis=1)
            part_a = standard.astype(BF16)
            left_over = standard - part_a.astype(F32)
            part_b = left_over.astype(BF16)
            part_c = (left_over - part_b.astype(F32)).astype(BF16)
            both = (
                jnp.dot(
                    w_bias, jnp.concatenate([part_a, part_b, part_c], axis=0), preferred_element_type=F32
                )
                * LOG2E
            )
            offsets += [both[:, :128], both[:, 128:]]
        for h in range(8):
            bias_block[h, g] = jnp.concatenate([v[h : h + 1] for v in offsets], axis=0)
        return carry

    lax.fori_loop(0, 4, outer_rest, 0)

    for h in range(2):
        for n in range(7):
            go(
                over_xz(
                    1 + h, n, bias_block.at[2 * to_xz(n) + h], bias.at[h, y, :, z, :, block_of(x)]
                )
            )
    own_bias = pltpu.make_async_copy(
        bias_block.at[pl.ds(2 * x, 2)], bias.at[:, y, :, z, :, block_of(x)], own.at[4]
    )
    own_bias.start()

    present = jnp.concatenate([r_all[32 + k, pl.ds(pl.multiple_of(16 * yz, 16), 16), :] for k in range(4)], axis=1).astype(F32) - 1.0
    penalty[...] = jnp.concatenate(
        [present * PENALTY[0], present * PENALTY[1], present * PENALTY[2], jnp.zeros((80, 512), F32)],
        axis=0,
    ).astype(BF16)

    def arrive_bias(h):
        for n in range(7):
            other_x, other_z = from_xz(n)
            over_xz(
                1 + h, n, bias_block.at[0], bias.at[h, y, :, other_z, :, block_of(other_x)]
            ).wait_recv()

    def bias_ring(h, c):
        def whole(b):
            return bias.at[h, b, pl.ds(2 * c, 2)]

        def half(b, way):
            return bias.at[h, b, 2 * c + way]

        number = 2 + 2 * h + c
        return Ring(where, whole, half, ring_send.at[number], ring_recv.at[number])

    r0, r1, r2, r3 = [bias_ring(h, c) for h in range(2) for c in range(2)]
    own_bias.wait()
    arrive_bias(0)
    r0.start()
    r1.start()
    arrive_bias(1)
    r2.start()
    r3.start()
    send_qkv(1, (2,))

    def attend(h, owner, blocks):
        count = 64 * len(blocks)
        lane = lax.broadcasted_iota(jnp.int32, (count, 128), 1)
        offset = jnp.concatenate([bias[h, b].reshape(64, 512) for b in blocks], axis=0)
        query = jnp.concatenate([qv[owner, h, 0, b].reshape(64, 128) for b in blocks], axis=0)
        every = qv[owner, h, 1].reshape(512, 128)
        weights, values = [], []
        for e in range(4):
            inside = groups == e
            keys = [jnp.zeros((32, 512), BF16)] * 4
            keys[e] = k_got[owner, h, 32 * e : 32 * e + 32, :]
            key = jnp.concatenate(keys + [penalty[...]], axis=0)
            value = jnp.where(inside, every, jnp.zeros((), BF16))
            values.append(jnp.concatenate([value, jnp.where(inside, 1.0, 0.0).astype(BF16)], axis=1))
            marked = (lax.rem(lane, 16) == owner * 4 + e) & (lane < 48)
            left = jnp.concatenate([query, jnp.where(marked, 1.0, 0.0).astype(BF16)], axis=1)
            scores = jnp.dot(left, key, preferred_element_type=F32) * SCORE_SCALE + offset
            top = jnp.max(scores, axis=-1, keepdims=True)
            weights.append(jnp.exp2(scores - top).astype(BF16))
        both = jnp.dot(
            jnp.concatenate(weights, axis=1),
            jnp.concatenate(values, axis=0),
            preferred_element_type=F32,
        )
        result = (both[:, :128] / both[:, 128:]).astype(BF16).reshape(len(blocks), 4, 16, 128)
        for k, b in enumerate(blocks):
            att_send[owner, h, b] = result[k]

    def run(h, offsets, after=()):
        blocks = [wrap(y + o, NY) for o in offsets]

        def body(n, carry):
            shift = jnp.where(n == 0, 2, jnp.where(n == 1, 1, jnp.where(n == 2, 3, 0)))
            attend(h, wrap(x + shift, NX), blocks)
            for k, action in enumerate(after):
                pl.when(n == k)(action)
            return carry

        lax.fori_loop(0, 4, body, 0)

    def turn_updated(g, carry):
        for i in range(8):
            pair_send[g, i] = updated_t[g, i].astype(F32).T.astype(BF16)
        return carry

    def back(h, n):
        return lambda: over_x(3 + h, n, att_send.at[to_x(n), h], att.at[x, h]).start()

    for copy in own_qkv:
        copy.wait()
    for n in range(3):
        arrive_qkv(0, n)
    run(0, (0,))
    r0.step(1)
    r1.step(1)
    lax.fori_loop(0, 4, turn_updated, 0)
    for n in range(3):
        go(over_x(2, n, pair_send.at[to_x(n)], out_pair.at[:, block_of(x), :]))
    own_pair = pltpu.make_async_copy(pair_send.at[x], out_pair.at[:, block_of(x), :], own.at[5])
    own_pair.start()
    r2.step(1)
    r3.step(1)
    run(0, (1, -1))
    r0.step(2)
    r1.step(2)
    for n in range(3):
        arrive_qkv(1, n)
    run(1, (0, 1, -1))
    r2.step(2)
    r3.step(2)
    run(0, (2, -2))
    r0.step(3)
    r1.step(3)
    run(1, (2, -2))
    r2.step(3)
    r3.step(3)
    r0.finish()
    r1.finish()
    run(0, (3, -3, 4), (back(0, 2), back(0, 0), back(0, 1)))
    r2.finish()
    r3.finish()
    run(1, (3, -3, 4), (back(1, 2), back(1, 0), back(1, 1)))
    own_att = pltpu.make_async_copy(att_send.at[x], att.at[x], own.at[6])
    own_att.start()
    own_att.wait()
    for h in range(2):
        for n in (2, 0, 1):
            over_x(3 + h, n, att_send.at[0, h], att.at[from_x(n), h]).wait_recv()
        for k in range(NX):
            out_gated[2 * k + h] = (att[k, h].reshape(512, 128).astype(F32) * gate[k, h]).astype(BF16)

    own_pair.wait()
    for n in range(3):
        over_x(2, n, pair_send.at[0], out_pair.at[:, block_of(from_x(n)), :]).wait_recv()
    for h in range(2):
        for n in range(3):
            over_x(3 + h, n, att_send.at[to_x(n), h], att.at[x, h]).wait_send()
    for copy in sent:
        copy.wait_send()
    for one in (near, rest, r0, r1, r2, r3):
        one.drain()


def finish(gated, hom, pair, w_final, out_hom, out_pair):
    out_pair[...] = pair[...]
    quads = [regroup(*[gated[4 * b + t].astype(F32) for t in range(4)]) for b in range(2)]
    joined = jnp.concatenate(
        [jnp.concatenate([quads[0][s], quads[1][s]], axis=1).astype(BF16) for s in range(4)], axis=0
    )
    update = jnp.dot(joined, w_final[...], preferred_element_type=F32)
    out_hom[...] = (hom[...].astype(F32) + update.reshape(4, 128, 256)).astype(BF16)


def on_device(
    homolog_tensor,
    couple_tensor,
    homolog_presence,
    asking_matrix,
    lookup_matrix,
    content_matrix,
    sigmoid_matrix,
    sigmoid_offset,
    attention_final_matrix,
    first_factor_matrix,
    second_factor_matrix,
    tensor_product_matrix,
    couple_offset_matrix,
):
    vmem = pl.BlockSpec(memory_space=pltpu.VMEM)
    dma = pltpu.SemaphoreType.DMA
    scratch = [
        pltpu.VMEM((4, 512, 256), BF16),
        pltpu.VMEM((16, 32, 128), BF16),
        pltpu.VMEM((4, 16, 32, 128), BF16),
        pltpu.VMEM((4, 4, ROWS, 128), BF16),
        pltpu.VMEM((2, 4, 4, ROWS, 128), BF16),
        pltpu.VMEM((32 * ROWS, 128), F32),
        pltpu.VMEM((PLANES, 256, 128), BF16),
        pltpu.VMEM((2048, 128), F32),
        pltpu.VMEM((1024, 256), BF16),
        pltpu.VMEM((1024, 256), BF16),
        pltpu.VMEM((1024, 128), F32),
        pltpu.VMEM((128, 1024), BF16),
        pltpu.VMEM((4, 2, 2, 8, 4, 16, 128), BF16),
        pltpu.VMEM((4, 2, 2, 8, 4, 16, 128), BF16),
        pltpu.VMEM((4, 2, 128, 512), BF16),
        pltpu.VMEM((4, 2, 128, 512), BF16),
        pltpu.VMEM((4, 2, 512, 128), F32),
        pltpu.VMEM((4, 8, 128, 128), BF16),
        pltpu.VMEM((4, 8, 128, 128), F32),
        pltpu.VMEM((4, 8, 128, 128), BF16),
        pltpu.VMEM((32, 128), F32),
        pltpu.VMEM((32, 1024, 128), BF16),
        pltpu.VMEM((4, 8, 128, 128), BF16),
        pltpu.VMEM((8, 4, 8, 128), F32),
        pltpu.VMEM((2, 8, 4, 2, 8, 512), F32),
        pltpu.VMEM((128, 512), BF16),
        pltpu.VMEM((4, 2, 8, 4, 16, 128), BF16),
        pltpu.VMEM((4, 2, 8, 4, 16, 128), BF16),
        dma((11, 3)),
        dma((11, 3)),
        dma((3, 7)),
        dma((3, 7)),
        dma((15,)),
        dma((15,)),
        dma((6, 2, 4)),
        dma((6, 2, 4)),
        dma((8,)),
    ]
    gated, pair = pl.pallas_call(
        kernel,
        name="evoformer_block",
        out_shape=(
            jax.ShapeDtypeStruct((8, 512, 128), BF16),
            jax.ShapeDtypeStruct((8, 512, 128), BF16),
        ),
        in_specs=[vmem] * 12,
        out_specs=(vmem, vmem),
        scratch_shapes=scratch,
        compiler_params=pltpu.CompilerParams(
            collective_id=1, has_side_effects=True, vmem_limit_bytes=60 << 20
        ),
    )(
        homolog_tensor,
        couple_tensor,
        homolog_presence,
        asking_matrix,
        lookup_matrix,
        content_matrix,
        sigmoid_matrix,
        sigmoid_offset.astype(F32).reshape(1, 256),
        first_factor_matrix.T,
        second_factor_matrix.T,
        tensor_product_matrix,
        couple_offset_matrix.T,
    )
    rows = lambda lead, width: pl.BlockSpec((lead, 128, width), lambda i: (0, i, 0))
    return pl.pallas_call(
        finish,
        name="final_projection",
        grid=(4,),
        out_shape=(
            jax.ShapeDtypeStruct((4, 512, 256), BF16),
            jax.ShapeDtypeStruct((8, 512, 128), BF16),
        ),
        in_specs=[
            rows(8, 128),
            rows(4, 256),
            rows(8, 128),
            pl.BlockSpec((256, 256), lambda i: (0, 0)),
        ],
        out_specs=(rows(4, 256), rows(8, 128)),
    )(gated, homolog_tensor, pair, attention_final_matrix)


def solution(mesh):
    return jax.shard_map(
        on_device,
        mesh=mesh,
        in_specs=(
            P(("dp", "dap"), None, None),
            P(("dp", "dap"), None, None),
            P(("dp", "dap"), None),
            P(),
            P(),
            P(),
            P(),
            P(),
            P(),
            P(),
            P(),
            P(),
            P(),
        ),
        out_specs=(P(("dp", "dap"), None, None), P(("dp", "dap"), None, None)),
        check_vma=False,
    )
```

```python
import functools
import math

import jax
import jax.numpy as jnp
from jax import lax
from jax.experimental import pallas as pl
from jax.experimental.pallas import tpu as pltpu
from jax.sharding import PartitionSpec as P

MESH = pl.DeviceIdType.MESH
F32 = jnp.float32
BF16 = jnp.bfloat16
LOG2E = math.log2(math.e)
SCORE_SCALE = 32.0**-0.5 * LOG2E
PENALTY = (56576.0, -7.46875, 0.01123046875)

NY, NX, NZ = 8, 4, 2
PLANES = 36
ROWS = 48
YZ_OFFSETS = [(dy, dz) for dz in range(NZ) for dy in range(NY) if (dy, dz) != (0, 0)]
X_OFFSETS = (1, 3, 2)
XZ_OFFSETS = [(dx, dz) for dx in (1, 3, 2, 0) for dz in range(NZ) if (dx, dz) != (0, 0)]


def wrap(value, size):
    return lax.rem(value + size, size)


def index_of(y, x, z):
    return (y * NX + x) * NZ + z


def remote(src, dst, send, recv, device):
    return pltpu.make_async_remote_copy(
        src_ref=src,
        dst_ref=dst,
        send_sem=send,
        recv_sem=recv,
        device_id={"dap": device},
        device_id_type=MESH,
    )


class Ring:
    def __init__(self, where, whole, half, send, recv):
        self.y, self.x, self.z = where
        self.whole, self.half = whole, half
        self.send, self.recv = send, recv

    def copy(self, way, step, block):
        view = self.half(block, way) if step == 3 else self.whole(block)
        to = wrap(self.y + (1 if way == 0 else -1), NY)
        return remote(
            view, view, self.send.at[way, step], self.recv.at[way, step], index_of(to, self.x, self.z)
        )

    def start(self):
        for way in (0, 1):
            self.copy(way, 0, self.y).start()

    def step(self, number):
        for way in (0, 1):
            block = wrap(self.y + (-number if way == 0 else number), NY)
            self.copy(way, number - 1, block).wait_recv()
            self.copy(way, number, block).start()

    def finish(self):
        for way in (0, 1):
            self.copy(way, 3, wrap(self.y + 4, NY)).wait_recv()

    def drain(self):
        for way in (0, 1):
            for step in range(4):
                self.copy(way, step, self.y).wait_send()


def regroup(v0, v1, v2, v3):
    lane = lax.broadcasted_iota(jnp.int32, v0.shape, 1)
    low = lane < 64
    even = lax.rem(lax.div(lane, 32), 2) == 0
    u0 = jnp.where(low, v0, pltpu.roll(v2, 64, 1))
    u2 = jnp.where(low, pltpu.roll(v0, 64, 1), v2)
    u1 = jnp.where(low, v1, pltpu.roll(v3, 64, 1))
    u3 = jnp.where(low, pltpu.roll(v1, 64, 1), v3)
    return (
        jnp.where(even, u0, pltpu.roll(u1, 32, 1)),
        jnp.where(even, pltpu.roll(u0, 96, 1), u1),
        jnp.where(even, u2, pltpu.roll(u3, 32, 1)),
        jnp.where(even, pltpu.roll(u2, 96, 1), u3),
    )


def perform(actions):
    for action in actions:
        action()


def normalize_rows(values):
    mean = jnp.mean(values, axis=-1, keepdims=True)
    centered = values - mean
    variance = jnp.mean(centered * centered, axis=-1, keepdims=True)
    return centered * lax.rsqrt(variance + 1e-05)


def nt_dot(left, right):
    return lax.dot_general(left, right, (((1,), (1,)), ((), ())), preferred_element_type=F32)


def kernel(
    hom,
    cpl,
    presence,
    w_query,
    w_key,
    w_value,
    w_gate,
    gate_offset,
    w_left_t,
    w_right_t,
    w_outer,
    w_bias_t,
    out_gated,
    out_pair,
    normed,
    l_send,
    l_all,
    r_send,
    r_got,
    r_wide,
    r_all,
    l_wide,
    l_mixed,
    l_t,
    w_outer_wide,
    w_outer_t,
    qv_send,
    qv,
    k_send,
    k_got,
    gate,
    couple,
    couple_t,
    updated_t,
    counts,
    outer,
    pair_send,
    bias_block,
    bias,
    penalty,
    att_send,
    att,
    x_send,
    x_recv,
    xz_send,
    xz_recv,
    yz_send,
    yz_recv,
    ring_send,
    ring_recv,
    own,
):
    me = lax.axis_index("dap")
    y = lax.div(me, NX * NZ)
    x = lax.rem(lax.div(me, NZ), NX)
    z = lax.rem(me, NZ)
    yz = y * NZ + z
    where = (y, x, z)

    barrier = pltpu.get_barrier_semaphore()
    for dx, dz in XZ_OFFSETS:
        if dx != 0:
            pl.semaphore_signal(
                barrier,
                inc=1,
                device_id={"dap": index_of(y, wrap(x + dx, NX), wrap(z + dz, NZ))},
                device_id_type=MESH,
            )
    for dy, dz in YZ_OFFSETS:
        pl.semaphore_signal(
            barrier,
            inc=1,
            device_id={"dap": index_of(wrap(y + dy, NY), x, wrap(z + dz, NZ))},
            device_id_type=MESH,
        )

    def over_x(kind, n, src, dst):
        to = index_of(y, wrap(x + X_OFFSETS[n], NX), z)
        return remote(src, dst, x_send.at[kind, n], x_recv.at[kind, n], to)

    def over_xz(kind, n, src, dst):
        dx, dz = XZ_OFFSETS[n]
        to = index_of(y, wrap(x + dx, NX), wrap(z + dz, NZ))
        return remote(src, dst, xz_send.at[kind, n], xz_recv.at[kind, n], to)

    def to_xz(n):
        return wrap(x + XZ_OFFSETS[n][0], NX)

    def from_xz(n):
        dx, dz = XZ_OFFSETS[n]
        return wrap(x - dx, NX), wrap(z - dz, NZ)

    def to_x(n):
        return wrap(x + X_OFFSETS[n], NX)

    def from_x(n):
        return wrap(x - X_OFFSETS[n], NX)

    sent = []

    def go(copy):
        copy.start()
        sent.append(copy)

    def block_of(k):
        return pl.ds(pl.multiple_of(128 * k, 128), 128)

    lanes = lax.broadcasted_iota(jnp.int32, (512, 128), 1)
    groups = lax.div(lanes, 32)

    def project_right(s, carry):
        lines = normalize_rows(hom[s].astype(F32)).astype(BF16)
        normed[s] = lines
        present = presence[pl.ds(s, 1), :].astype(F32)
        right = (nt_dot(w_right_t[...], lines) * present).astype(BF16)
        rows = jnp.concatenate(
            [present[:, 128 * k : 128 * k + 128] for k in range(4)] + [jnp.zeros((12, 128), F32)], axis=0
        ).astype(BF16)
        for k in range(NX):
            r_send[k, s, 0:32, :] = right[:, 128 * k : 128 * k + 128]
            r_send[k, s, 32:48, :] = rows
        return carry

    lax.fori_loop(0, 4, project_right, 0)
    pl.semaphore_wait(barrier, 6 + len(YZ_OFFSETS))
    for n in range(7):
        go(over_xz(0, n, r_send.at[to_xz(n)], r_got.at[z, x]))

    w_left = jnp.concatenate([w_left_t[...]] * 4, axis=0)

    def project_left(s, total):
        return jnp.where(groups == s, nt_dot(normed[s], w_left), total)

    left = lax.fori_loop(0, 4, project_left, jnp.zeros((512, 128), F32))
    spread = jnp.where(
        lax.div(lax.broadcasted_iota(jnp.int32, (128, 128), 1), 32)
        == lax.broadcasted_iota(jnp.int32, (128, 128), 0),
        1.0,
        0.0,
    ).astype(BF16)
    tall = jnp.concatenate([presence[...].astype(F32), jnp.zeros((124, 512), F32)], axis=0).T
    left = left * jnp.dot(tall.astype(BF16), spread, preferred_element_type=F32)
    left = left.reshape(NY, NX, NZ, 8, 128)
    for b in range(NY):
        for c in range(NZ):
            l_send[b * NZ + c] = left[b, :, c].reshape(32, 128).astype(BF16)

    for n, (dy, dz) in enumerate(YZ_OFFSETS):
        to_y, to_z = wrap(y + dy, NY), wrap(z + dz, NZ)
        go(
            remote(
                l_send.at[to_y * NZ + to_z],
                l_all.at[x, yz],
                yz_send.at[n],
                yz_recv.at[n],
                index_of(to_y, x, to_z),
            )
        )
    for n in range(3):
        go(over_x(1, n, cpl.at[:, block_of(to_x(n)), :], couple.at[x]))
    own_copies = [
        pltpu.make_async_copy(r_send.at[x], r_got.at[z, x], own.at[0]),
        pltpu.make_async_copy(l_send.at[yz], l_all.at[x, yz], own.at[1]),
        pltpu.make_async_copy(cpl.at[:, block_of(x), :], couple.at[x], own.at[2]),
    ]
    for copy in own_copies:
        copy.start()

    def heads(part, carry):
        rows = pl.ds(pl.multiple_of(128 * part, 128), 128)
        for kind, w in enumerate((w_query, w_value, w_gate)):
            made = [jnp.dot(normed[s, rows, :], w[...], preferred_element_type=F32) for s in range(4)]
            if kind == 2:
                made = [jax.nn.sigmoid(m + offset_row) for m in made]
            for b in range(2):
                outs = regroup(*[m[:, 128 * b : 128 * b + 128] for m in made])
                for t in range(4):
                    h = 4 * b + t
                    if kind == 2:
                        gate[h // 2, h % 2, rows, :] = outs[t]
                    else:
                        qv_send[h // 2, h % 2, kind, pl.ds(2 * part, 2)] = (
                            outs[t].astype(BF16).reshape(2, 4, 16, 128)
                        )
        return carry

    offset_row = gate_offset[...].astype(F32).reshape(1, 256)
    w_key_t = w_key[...].astype(F32).T.astype(BF16)

    def keys(s, carry):
        made = nt_dot(w_key_t, normed[s]).astype(BF16)
        for h in range(8):
            k_send[h // 2, h % 2, pl.ds(pl.multiple_of(32 * s, 32), 32), :] = made[32 * h : 32 * h + 32]
        return carry

    lax.fori_loop(0, 4, keys, 0)
    lax.fori_loop(0, 4, heads, 0)

    def qkv_copies(h, n):
        other = from_x(n)
        return (
            (5 + 3 * h, k_send.at[to_x(n), h], k_got.at[x, h], k_got.at[other, h]),
            (6 + 3 * h, qv_send.at[to_x(n), h, 1], qv.at[x, h, 1], qv.at[other, h, 1]),
            (7 + 3 * h, qv_send.at[to_x(n), h, 0], qv.at[x, h, 0], qv.at[other, h, 0]),
        )

    def send_qkv(h, kinds=(0, 1, 2)):
        for k in kinds:
            for n in range(3):
                kind, src, dst, _ = qkv_copies(h, n)[k]
                go(over_x(kind, n, src, dst))

    def arrive_qkv(h, n):
        for kind, src, _, got in qkv_copies(h, n):
            over_x(kind, n, src, got).wait_recv()

    own_qkv = [
        pltpu.make_async_copy(k_send.at[x], k_got.at[x], own.at[3]),
        pltpu.make_async_copy(qv_send.at[x], qv.at[x], own.at[7]),
    ]
    for copy in own_qkv:
        copy.start()

    own_copies[0].wait()
    for n in range(7):
        other_x, other_z = from_xz(n)
        over_xz(0, n, r_send.at[0], r_got.at[other_z, other_x]).wait_recv()
    r_wide[...] = r_got[...].astype(F32).reshape(32 * ROWS, 128)

    def line_of(b):
        return pl.ds(pl.multiple_of(32 * b, 32), 32)

    for q in range(PLANES):
        r_all[q, line_of(y), :] = r_wide[pl.ds(q, 32, stride=ROWS), :].astype(BF16)

    def right_ring(c):
        first = (0, 18)[c]

        def whole(b):
            return r_all.at[pl.ds(first, 18), line_of(b), :]

        def half(b, way):
            return r_all.at[pl.ds(first + 9 * way, 9), line_of(b), :]

        return Ring(where, whole, half, ring_send.at[c], ring_recv.at[c])

    near, rest = right_ring(0), right_ring(1)
    near.start()
    rest.start()

    own_copies[1].wait()
    for n, (dy, dz) in enumerate(YZ_OFFSETS):
        from_yz = wrap(y - dy, NY) * NZ + wrap(z - dz, NZ)
        remote(l_send.at[0], l_all.at[x, from_yz], yz_send.at[n], yz_recv.at[n], me).wait_recv()
    for n in range(3):
        go(over_x(0, n, l_all.at[x], l_all.at[x]))
    send_qkv(0)

    near.step(1)
    rest.step(1)

    w_outer_wide[...] = w_outer[...].astype(F32)
    for k in range(8):
        w_outer_t[:, 128 * k : 128 * k + 128] = (
            jnp.concatenate([w_outer_wide[pl.ds(4 * k + t, 32, stride=32), :] for t in range(4)], axis=0)
            .T.astype(BF16)
        )

    near.step(2)
    rest.step(2)

    for n in range(3):
        over_x(0, n, l_all.at[x], l_all.at[from_x(n)]).wait_recv()
    l_wide[...] = l_all[...].astype(F32).reshape(2048, 128)
    for pair in range(16):
        block = jnp.concatenate(
            [l_wide[pl.ds(2 * pair, 64, stride=32), :], l_wide[pl.ds(2 * pair + 1, 64, stride=32), :]],
            axis=0,
        ).T
        for e in range(2):
            l_mixed[pl.ds((2 * pair + e) * 32, 32), :] = jnp.concatenate(
                [block[32 * s : 32 * s + 32, 64 * e : 64 * e + 64] for s in range(4)], axis=1
            ).astype(BF16)
    source = lax.broadcasted_iota(jnp.int32, (256, 256), 0)
    target = lax.broadcasted_iota(jnp.int32, (256, 256), 1)
    place = lax.rem(source, 16) * 16 + lax.rem(lax.div(source, 16), 4) * 4 + lax.div(source, 64)
    order = jnp.where(place == target, 1.0, 0.0).astype(BF16)
    l_t[...] = jnp.dot(l_mixed[...], order, preferred_element_type=F32).astype(BF16)

    own_copies[2].wait()
    for n in range(3):
        over_x(1, n, cpl.at[:, pl.ds(0, 128), :], couple.at[from_x(n)]).wait_recv()

    def turn_couple(g, carry):
        for i in range(8):
            couple_t[g, i] = couple[g, i].astype(F32).T
        return carry

    lax.fori_loop(0, 4, turn_couple, 0)
    near.step(3)
    send_qkv(1, (0, 1))
    rest.step(3)
    near.finish()

    def outer_rows(g, first, last):
        l_rows = l_t[pl.ds(pl.multiple_of(g * 256, 256), 256), :]
        for d in range(first, last):
            right = jnp.concatenate([r_all[2 * d], r_all[2 * d + 1]], axis=1)
            product = jnp.dot(l_rows, right, preferred_element_type=F32).astype(BF16)
            for e in range(2):
                outer[pl.ds(8 * g, 8), (2 * d + e) * 32 : (2 * d + e) * 32 + 32, :] = product[
                    :, 128 * e : 128 * e + 128
                ].reshape(8, 32, 128)

    def outer_near(g, carry):
        outer_rows(g, 0, 9)
        return carry

    lax.fori_loop(0, 4, outer_near, 0)
    rest.finish()

    plane = r_all[32 + lax.div(y, 2)].astype(F32).T.astype(BF16)
    together = jnp.dot(plane, r_all[32 + x], preferred_element_type=F32).astype(BF16)
    row = lax.broadcasted_iota(jnp.int32, (32, 128), 0)
    column = lax.broadcasted_iota(jnp.int32, (32, 128), 1)
    chosen = 64 * lax.rem(y, 2) + 16 * lax.div(row, 8) + 8 * z + lax.rem(row, 8)
    pick = jnp.where(chosen == column, 1.0, 0.0).astype(BF16)
    counts[...] = 1.0 / (jnp.dot(pick, together, preferred_element_type=F32) + 0.001)

    w_bias = jnp.concatenate([w_bias_t[...]] * 3, axis=1)

    def outer_rest(g, carry):
        outer_rows(g, 9, 16)
        offsets = []
        for pair in range(4):
            right = jnp.concatenate([outer[8 * g + 2 * pair], outer[8 * g + 2 * pair + 1]], axis=1)
            update = jnp.dot(w_outer_t[...], right, preferred_element_type=F32)
            standards = []
            for e in range(2):
                i = 2 * pair + e
                scaled = update[:, 128 * e : 128 * e + 128] * counts[pl.ds(g * 8 + i, 1), :]
                updated = (couple_t[g, i] + scaled).astype(BF16)
                updated_t[g, i] = updated
                updated = updated.astype(F32)
                mean = jnp.mean(updated, axis=0, keepdims=True)
                centered = updated - mean
                variance = jnp.mean(centered * centered, axis=0, keepdims=True)
                standards.append(centered * lax.rsqrt(variance + 1e-05))
            standard = jnp.concatenate(standards, axis=1)
            part_a = standard.astype(BF16)
            left_over = standard - part_a.astype(F32)
            part_b = left_over.astype(BF16)
            part_c = (left_over - part_b.astype(F32)).astype(BF16)
            both = (
                jnp.dot(
                    w_bias, jnp.concatenate([part_a, part_b, part_c], axis=0), preferred_element_type=F32
                )
                * LOG2E
            )
            offsets += [both[:, :128], both[:, 128:]]
        for h in range(8):
            bias_block[h, g] = jnp.concatenate([v[h : h + 1] for v in offsets], axis=0)
        return carry

    def send_bias(c):
        half_rows = pl.ds(2 * c, 2)
        for h in range(2):
            for n in range(7):
                go(
                    over_xz(
                        1 + 2 * c + h,
                        n,
                        bias_block.at[2 * to_xz(n) + h, half_rows],
                        bias.at[h, y, half_rows, z, :, block_of(x)],
                    )
                )
        copy = pltpu.make_async_copy(
            bias_block.at[pl.ds(2 * x, 2), half_rows],
            bias.at[:, y, half_rows, z, :, block_of(x)],
            own.at[(4, 8)[c]],
        )
        copy.start()
        return copy

    lax.fori_loop(0, 2, outer_rest, 0)
    own_bias = [send_bias(0)]
    lax.fori_loop(2, 4, outer_rest, 0)
    own_bias.append(send_bias(1))

    present = jnp.concatenate([r_all[32 + k, pl.ds(pl.multiple_of(16 * yz, 16), 16), :] for k in range(4)], axis=1).astype(F32) - 1.0
    penalty[...] = jnp.concatenate(
        [present * PENALTY[0], present * PENALTY[1], present * PENALTY[2], jnp.zeros((80, 512), F32)],
        axis=0,
    ).astype(BF16)

    def arrive_bias(c):
        half_rows = pl.ds(2 * c, 2)
        own_bias[c].wait()
        for h in range(2):
            for n in range(7):
                other_x, other_z = from_xz(n)
                over_xz(
                    1 + 2 * c + h,
                    n,
                    bias_block.at[0, half_rows],
                    bias.at[h, y, half_rows, other_z, :, block_of(other_x)],
                ).wait_recv()

    def bias_ring(h, c):
        def whole(b):
            return bias.at[h, b, pl.ds(2 * c, 2)]

        def half(b, way):
            return bias.at[h, b, 2 * c + way]

        number = 2 + 2 * h + c
        return Ring(where, whole, half, ring_send.at[number], ring_recv.at[number])

    r0, r1, r2, r3 = [bias_ring(h, c) for h in range(2) for c in range(2)]
    arrive_bias(0)
    r0.start()
    r2.start()
    arrive_bias(1)
    r1.start()
    r3.start()
    send_qkv(1, (2,))

    def attend(h, owner, blocks):
        count = 64 * len(blocks)
        lane = lax.broadcasted_iota(jnp.int32, (count, 128), 1)
        offset = jnp.concatenate([bias[h, b].reshape(64, 512) for b in blocks], axis=0)
        query = jnp.concatenate([qv[owner, h, 0, b].reshape(64, 128) for b in blocks], axis=0)
        every = qv[owner, h, 1].reshape(512, 128)
        weights, values = [], []
        for e in range(4):
            inside = groups == e
            keys = [jnp.zeros((32, 512), BF16)] * 4
            keys[e] = k_got[owner, h, 32 * e : 32 * e + 32, :]
            key = jnp.concatenate(keys + [penalty[...]], axis=0)
            value = jnp.where(inside, every, jnp.zeros((), BF16))
            values.append(jnp.concatenate([value, jnp.where(inside, 1.0, 0.0).astype(BF16)], axis=1))
            marked = (lax.rem(lane, 16) == owner * 4 + e) & (lane < 48)
            left = jnp.concatenate([query, jnp.where(marked, 1.0, 0.0).astype(BF16)], axis=1)
            scores = jnp.dot(left, key, preferred_element_type=F32) * SCORE_SCALE + offset
            top = jnp.max(scores, axis=-1, keepdims=True)
            weights.append(jnp.exp2(scores - top).astype(BF16))
        both = jnp.dot(
            jnp.concatenate(weights, axis=1),
            jnp.concatenate(values, axis=0),
            preferred_element_type=F32,
        )
        result = (both[:, :128] / both[:, 128:]).astype(BF16).reshape(len(blocks), 4, 16, 128)
        for k, b in enumerate(blocks):
            att_send[owner, h, b] = result[k]

    def run(h, offsets, after=()):
        blocks = [wrap(y + o, NY) for o in offsets]

        def body(n, carry):
            shift = jnp.where(n == 0, 2, jnp.where(n == 1, 1, jnp.where(n == 2, 3, 0)))
            attend(h, wrap(x + shift, NX), blocks)
            for k, action in enumerate(after):
                pl.when(n == k)(action)
            return carry

        lax.fori_loop(0, 4, body, 0)

    def turn_updated(g, carry):
        for i in range(8):
            pair_send[g, i] = updated_t[g, i].astype(F32).T.astype(BF16)
        return carry

    def back(h, n):
        return lambda: over_x(3 + h, n, att_send.at[to_x(n), h], att.at[x, h]).start()

    for copy in own_qkv:
        copy.wait()
    for n in range(3):
        arrive_qkv(0, n)
    run(0, (0,))
    r0.step(1)
    r1.step(1)
    lax.fori_loop(0, 4, turn_updated, 0)
    for n in range(3):
        go(over_x(2, n, pair_send.at[to_x(n)], out_pair.at[:, block_of(x), :]))
    own_pair = pltpu.make_async_copy(pair_send.at[x], out_pair.at[:, block_of(x), :], own.at[5])
    own_pair.start()
    r2.step(1)
    r3.step(1)
    run(0, (1, -1))
    r0.step(2)
    r1.step(2)
    for n in range(3):
        arrive_qkv(1, n)
    run(1, (0, 1, -1))
    r2.step(2)
    r3.step(2)
    run(0, (2, -2))
    r0.step(3)
    r1.step(3)
    run(1, (2, -2))
    r2.step(3)
    r3.step(3)
    r0.finish()
    r1.finish()
    run(0, (3, -3, 4), (back(0, 2), back(0, 0), back(0, 1)))
    r2.finish()
    r3.finish()
    run(1, (3, -3, 4), (back(1, 2), back(1, 0), back(1, 1)))
    own_att = pltpu.make_async_copy(att_send.at[x], att.at[x], own.at[6])
    own_att.start()
    own_att.wait()
    for h in range(2):
        for n in (2, 0, 1):
            over_x(3 + h, n, att_send.at[0, h], att.at[from_x(n), h]).wait_recv()
        for k in range(NX):
            out_gated[2 * k + h] = (att[k, h].reshape(512, 128).astype(F32) * gate[k, h]).astype(BF16)

    own_pair.wait()
    for n in range(3):
        over_x(2, n, pair_send.at[0], out_pair.at[:, block_of(from_x(n)), :]).wait_recv()
    for h in range(2):
        for n in range(3):
            over_x(3 + h, n, att_send.at[to_x(n), h], att.at[x, h]).wait_send()
    for copy in sent:
        copy.wait_send()
    for one in (near, rest, r0, r1, r2, r3):
        one.drain()


def finish(gated, hom, pair, w_final, out_hom, out_pair):
    out_pair[...] = pair[...]
    quads = [regroup(*[gated[4 * b + t].astype(F32) for t in range(4)]) for b in range(2)]
    joined = jnp.concatenate(
        [jnp.concatenate([quads[0][s], quads[1][s]], axis=1).astype(BF16) for s in range(4)], axis=0
    )
    update = jnp.dot(joined, w_final[...], preferred_element_type=F32)
    out_hom[...] = (hom[...].astype(F32) + update.reshape(4, 128, 256)).astype(BF16)


def on_device(
    homolog_tensor,
    couple_tensor,
    homolog_presence,
    asking_matrix,
    lookup_matrix,
    content_matrix,
    sigmoid_matrix,
    sigmoid_offset,
    attention_final_matrix,
    first_factor_matrix,
    second_factor_matrix,
    tensor_product_matrix,
    couple_offset_matrix,
):
    vmem = pl.BlockSpec(memory_space=pltpu.VMEM)
    dma = pltpu.SemaphoreType.DMA
    scratch = [
        pltpu.VMEM((4, 512, 256), BF16),
        pltpu.VMEM((16, 32, 128), BF16),
        pltpu.VMEM((4, 16, 32, 128), BF16),
        pltpu.VMEM((4, 4, ROWS, 128), BF16),
        pltpu.VMEM((2, 4, 4, ROWS, 128), BF16),
        pltpu.VMEM((32 * ROWS, 128), F32),
        pltpu.VMEM((PLANES, 256, 128), BF16),
        pltpu.VMEM((2048, 128), F32),
        pltpu.VMEM((1024, 256), BF16),
        pltpu.VMEM((1024, 256), BF16),
        pltpu.VMEM((1024, 128), F32),
        pltpu.VMEM((128, 1024), BF16),
        pltpu.VMEM((4, 2, 2, 8, 4, 16, 128), BF16),
        pltpu.VMEM((4, 2, 2, 8, 4, 16, 128), BF16),
        pltpu.VMEM((4, 2, 128, 512), BF16),
        pltpu.VMEM((4, 2, 128, 512), BF16),
        pltpu.VMEM((4, 2, 512, 128), F32),
        pltpu.VMEM((4, 8, 128, 128), BF16),
        pltpu.VMEM((4, 8, 128, 128), F32),
        pltpu.VMEM((4, 8, 128, 128), BF16),
        pltpu.VMEM((32, 128), F32),
        pltpu.VMEM((32, 1024, 128), BF16),
        pltpu.VMEM((4, 8, 128, 128), BF16),
        pltpu.VMEM((8, 4, 8, 128), F32),
        pltpu.VMEM((2, 8, 4, 2, 8, 512), F32),
        pltpu.VMEM((128, 512), BF16),
        pltpu.VMEM((4, 2, 8, 4, 16, 128), BF16),
        pltpu.VMEM((4, 2, 8, 4, 16, 128), BF16),
        dma((11, 3)),
        dma((11, 3)),
        dma((5, 7)),
        dma((5, 7)),
        dma((15,)),
        dma((15,)),
        dma((6, 2, 4)),
        dma((6, 2, 4)),
        dma((9,)),
    ]
    gated, pair = pl.pallas_call(
        kernel,
        name="evoformer_block",
        out_shape=(
            jax.ShapeDtypeStruct((8, 512, 128), BF16),
            jax.ShapeDtypeStruct((8, 512, 128), BF16),
        ),
        in_specs=[vmem] * 12,
        out_specs=(vmem, vmem),
        scratch_shapes=scratch,
        compiler_params=pltpu.CompilerParams(
            collective_id=1, has_side_effects=True, vmem_limit_bytes=60 << 20
        ),
    )(
        homolog_tensor,
        couple_tensor,
        homolog_presence,
        asking_matrix,
        lookup_matrix,
        content_matrix,
        sigmoid_matrix,
        sigmoid_offset,
        first_factor_matrix.T,
        second_factor_matrix.T,
        tensor_product_matrix,
        couple_offset_matrix.T,
    )
    rows = lambda lead, width: pl.BlockSpec((lead, 128, width), lambda i: (0, i, 0))
    return pl.pallas_call(
        finish,
        name="final_projection",
        grid=(4,),
        out_shape=(
            jax.ShapeDtypeStruct((4, 512, 256), BF16),
            jax.ShapeDtypeStruct((8, 512, 128), BF16),
        ),
        in_specs=[
            rows(8, 128),
            rows(4, 256),
            rows(8, 128),
            pl.BlockSpec((256, 256), lambda i: (0, 0)),
        ],
        out_specs=(rows(4, 256), rows(8, 128)),
    )(gated, homolog_tensor, pair, attention_final_matrix)


def solution(mesh):
    return jax.shard_map(
        on_device,
        mesh=mesh,
        in_specs=(
            P(("dp", "dap"), None, None),
            P(("dp", "dap"), None, None),
            P(("dp", "dap"), None),
            P(),
            P(),
            P(),
            P(),
            P(),
            P(),
            P(),
            P(),
            P(),
            P(),
        ),
        out_specs=(P(("dp", "dap"), None, None), P(("dp", "dap"), None, None)),
        check_vma=False,
    )
```

```python
import functools
import math

import jax
import jax.numpy as jnp
from jax import lax
from jax.experimental import pallas as pl
from jax.experimental.pallas import tpu as pltpu
from jax.sharding import PartitionSpec as P

MESH = pl.DeviceIdType.MESH
F32 = jnp.float32
BF16 = jnp.bfloat16
LOG2E = math.log2(math.e)
SCORE_SCALE = 32.0**-0.5 * LOG2E
PENALTY = (56576.0, -7.46875, 0.01123046875)

NY, NX, NZ = 8, 4, 2
PLANES = 36
ROWS = 48
YZ_OFFSETS = [(dy, dz) for dz in range(NZ) for dy in range(NY) if (dy, dz) != (0, 0)]
X_OFFSETS = (1, 3, 2)
XZ_OFFSETS = [(dx, dz) for dx in (1, 3, 2, 0) for dz in range(NZ) if (dx, dz) != (0, 0)]


def wrap(value, size):
    return lax.rem(value + size, size)


def index_of(y, x, z):
    return (y * NX + x) * NZ + z


def remote(src, dst, send, recv, device):
    return pltpu.make_async_remote_copy(
        src_ref=src,
        dst_ref=dst,
        send_sem=send,
        recv_sem=recv,
        device_id={"dap": device},
        device_id_type=MESH,
    )


class Ring:
    def __init__(self, where, whole, half, send, recv):
        self.y, self.x, self.z = where
        self.whole, self.half = whole, half
        self.send, self.recv = send, recv

    def copy(self, way, step, block):
        view = self.half(block, way) if step == 3 else self.whole(block)
        to = wrap(self.y + (1 if way == 0 else -1), NY)
        return remote(
            view, view, self.send.at[way, step], self.recv.at[way, step], index_of(to, self.x, self.z)
        )

    def start(self):
        for way in (0, 1):
            self.copy(way, 0, self.y).start()

    def step(self, number):
        for way in (0, 1):
            block = wrap(self.y + (-number if way == 0 else number), NY)
            self.copy(way, number - 1, block).wait_recv()
            self.copy(way, number, block).start()

    def finish(self):
        for way in (0, 1):
            self.copy(way, 3, wrap(self.y + 4, NY)).wait_recv()

    def drain(self):
        for way in (0, 1):
            for step in range(4):
                self.copy(way, step, self.y).wait_send()


def regroup(v0, v1, v2, v3):
    lane = lax.broadcasted_iota(jnp.int32, v0.shape, 1)
    low = lane < 64
    even = lax.rem(lax.div(lane, 32), 2) == 0
    u0 = jnp.where(low, v0, pltpu.roll(v2, 64, 1))
    u2 = jnp.where(low, pltpu.roll(v0, 64, 1), v2)
    u1 = jnp.where(low, v1, pltpu.roll(v3, 64, 1))
    u3 = jnp.where(low, pltpu.roll(v1, 64, 1), v3)
    return (
        jnp.where(even, u0, pltpu.roll(u1, 32, 1)),
        jnp.where(even, pltpu.roll(u0, 96, 1), u1),
        jnp.where(even, u2, pltpu.roll(u3, 32, 1)),
        jnp.where(even, pltpu.roll(u2, 96, 1), u3),
    )


def perform(actions):
    for action in actions:
        action()


def normalize_rows(values):
    mean = jnp.mean(values, axis=-1, keepdims=True)
    centered = values - mean
    variance = jnp.mean(centered * centered, axis=-1, keepdims=True)
    return centered * lax.rsqrt(variance + 1e-05)


def nt_dot(left, right):
    return lax.dot_general(left, right, (((1,), (1,)), ((), ())), preferred_element_type=F32)


def kernel(
    hom,
    cpl,
    presence,
    w_query,
    w_key,
    w_value,
    w_gate,
    gate_offset,
    w_left_t,
    w_right_t,
    w_outer,
    w_bias_t,
    out_gated,
    out_pair,
    normed,
    l_send,
    l_all,
    r_send,
    r_got,
    r_wide,
    r_all,
    l_wide,
    l_mixed,
    l_t,
    w_outer_wide,
    w_outer_t,
    qv_send,
    qv,
    k_send,
    k_got,
    gate,
    couple,
    couple_t,
    updated_t,
    counts,
    outer,
    pair_send,
    bias_block,
    bias,
    penalty,
    att_send,
    att,
    x_send,
    x_recv,
    xz_send,
    xz_recv,
    yz_send,
    yz_recv,
    ring_send,
    ring_recv,
    att_out,
    att_in,
    own,
):
    me = lax.axis_index("dap")
    y = lax.div(me, NX * NZ)
    x = lax.rem(lax.div(me, NZ), NX)
    z = lax.rem(me, NZ)
    yz = y * NZ + z
    where = (y, x, z)

    barrier = pltpu.get_barrier_semaphore()
    for dx, dz in XZ_OFFSETS:
        if dx != 0:
            pl.semaphore_signal(
                barrier,
                inc=1,
                device_id={"dap": index_of(y, wrap(x + dx, NX), wrap(z + dz, NZ))},
                device_id_type=MESH,
            )
    for dy, dz in YZ_OFFSETS:
        pl.semaphore_signal(
            barrier,
            inc=1,
            device_id={"dap": index_of(wrap(y + dy, NY), x, wrap(z + dz, NZ))},
            device_id_type=MESH,
        )

    def over_x(kind, n, src, dst):
        to = index_of(y, wrap(x + X_OFFSETS[n], NX), z)
        return remote(src, dst, x_send.at[kind, n], x_recv.at[kind, n], to)

    def over_xz(kind, n, src, dst):
        dx, dz = XZ_OFFSETS[n]
        to = index_of(y, wrap(x + dx, NX), wrap(z + dz, NZ))
        return remote(src, dst, xz_send.at[kind, n], xz_recv.at[kind, n], to)

    def to_xz(n):
        return wrap(x + XZ_OFFSETS[n][0], NX)

    def from_xz(n):
        dx, dz = XZ_OFFSETS[n]
        return wrap(x - dx, NX), wrap(z - dz, NZ)

    def to_x(n):
        return wrap(x + X_OFFSETS[n], NX)

    def from_x(n):
        return wrap(x - X_OFFSETS[n], NX)

    sent = []

    def go(copy):
        copy.start()
        sent.append(copy)

    def block_of(k):
        return pl.ds(pl.multiple_of(128 * k, 128), 128)

    lanes = lax.broadcasted_iota(jnp.int32, (512, 128), 1)
    groups = lax.div(lanes, 32)

    def project_right(s, carry):
        lines = normalize_rows(hom[s].astype(F32)).astype(BF16)
        normed[s] = lines
        present = presence[pl.ds(s, 1), :].astype(F32)
        right = (nt_dot(w_right_t[...], lines) * present).astype(BF16)
        rows = jnp.concatenate(
            [present[:, 128 * k : 128 * k + 128] for k in range(4)] + [jnp.zeros((12, 128), F32)], axis=0
        ).astype(BF16)
        for k in range(NX):
            r_send[k, s, 0:32, :] = right[:, 128 * k : 128 * k + 128]
            r_send[k, s, 32:48, :] = rows
        return carry

    lax.fori_loop(0, 4, project_right, 0)
    pl.semaphore_wait(barrier, 6 + len(YZ_OFFSETS))
    for n in range(7):
        go(over_xz(0, n, r_send.at[to_xz(n)], r_got.at[z, x]))

    w_left = jnp.concatenate([w_left_t[...]] * 4, axis=0)

    def project_left(s, total):
        return jnp.where(groups == s, nt_dot(normed[s], w_left), total)

    left = lax.fori_loop(0, 4, project_left, jnp.zeros((512, 128), F32))
    spread = jnp.where(
        lax.div(lax.broadcasted_iota(jnp.int32, (128, 128), 1), 32)
        == lax.broadcasted_iota(jnp.int32, (128, 128), 0),
        1.0,
        0.0,
    ).astype(BF16)
    tall = jnp.concatenate([presence[...].astype(F32), jnp.zeros((124, 512), F32)], axis=0).T
    left = left * jnp.dot(tall.astype(BF16), spread, preferred_element_type=F32)
    left = left.reshape(NY, NX, NZ, 8, 128)
    for b in range(NY):
        for c in range(NZ):
            l_send[b * NZ + c] = left[b, :, c].reshape(32, 128).astype(BF16)

    for n, (dy, dz) in enumerate(YZ_OFFSETS):
        to_y, to_z = wrap(y + dy, NY), wrap(z + dz, NZ)
        go(
            remote(
                l_send.at[to_y * NZ + to_z],
                l_all.at[x, yz],
                yz_send.at[n],
                yz_recv.at[n],
                index_of(to_y, x, to_z),
            )
        )
    for n in range(3):
        go(over_x(1, n, cpl.at[:, block_of(to_x(n)), :], couple.at[x]))
    own_copies = [
        pltpu.make_async_copy(r_send.at[x], r_got.at[z, x], own.at[0]),
        pltpu.make_async_copy(l_send.at[yz], l_all.at[x, yz], own.at[1]),
        pltpu.make_async_copy(cpl.at[:, block_of(x), :], couple.at[x], own.at[2]),
    ]
    for copy in own_copies:
        copy.start()

    def heads(part, carry):
        rows = pl.ds(pl.multiple_of(128 * part, 128), 128)
        for kind, w in enumerate((w_query, w_value, w_gate)):
            made = [jnp.dot(normed[s, rows, :], w[...], preferred_element_type=F32) for s in range(4)]
            if kind == 2:
                made = [jax.nn.sigmoid(m + offset_row) for m in made]
            for b in range(2):
                outs = regroup(*[m[:, 128 * b : 128 * b + 128] for m in made])
                for t in range(4):
                    h = 4 * b + t
                    if kind == 2:
                        gate[h // 2, h % 2, rows, :] = outs[t]
                    else:
                        qv_send[h // 2, h % 2, kind, pl.ds(2 * part, 2)] = (
                            outs[t].astype(BF16).reshape(2, 4, 16, 128)
                        )
        return carry

    offset_row = gate_offset[...].astype(F32).reshape(1, 256)
    w_key_t = w_key[...].astype(F32).T.astype(BF16)

    def keys(s, carry):
        made = nt_dot(w_key_t, normed[s]).astype(BF16)
        for h in range(8):
            k_send[h // 2, h % 2, pl.ds(pl.multiple_of(32 * s, 32), 32), :] = made[32 * h : 32 * h + 32]
        return carry

    lax.fori_loop(0, 4, keys, 0)
    lax.fori_loop(0, 4, heads, 0)

    def qkv_copies(h, n):
        other = from_x(n)
        return (
            (5 + 3 * h, k_send.at[to_x(n), h], k_got.at[x, h], k_got.at[other, h]),
            (6 + 3 * h, qv_send.at[to_x(n), h, 1], qv.at[x, h, 1], qv.at[other, h, 1]),
            (7 + 3 * h, qv_send.at[to_x(n), h, 0], qv.at[x, h, 0], qv.at[other, h, 0]),
        )

    def send_qkv(h, kinds=(0, 1, 2)):
        for k in kinds:
            for n in range(3):
                kind, src, dst, _ = qkv_copies(h, n)[k]
                go(over_x(kind, n, src, dst))

    def arrive_qkv(h, n):
        for kind, src, _, got in qkv_copies(h, n):
            over_x(kind, n, src, got).wait_recv()

    own_qkv = [
        pltpu.make_async_copy(k_send.at[x], k_got.at[x], own.at[3]),
        pltpu.make_async_copy(qv_send.at[x], qv.at[x], own.at[7]),
    ]
    for copy in own_qkv:
        copy.start()

    own_copies[0].wait()
    for n in range(7):
        other_x, other_z = from_xz(n)
        over_xz(0, n, r_send.at[0], r_got.at[other_z, other_x]).wait_recv()
    r_wide[...] = r_got[...].astype(F32).reshape(32 * ROWS, 128)

    def line_of(b):
        return pl.ds(pl.multiple_of(32 * b, 32), 32)

    for q in range(PLANES):
        r_all[q, line_of(y), :] = r_wide[pl.ds(q, 32, stride=ROWS), :].astype(BF16)

    def right_ring(c):
        first = (0, 18)[c]

        def whole(b):
            return r_all.at[pl.ds(first, 18), line_of(b), :]

        def half(b, way):
            return r_all.at[pl.ds(first + 9 * way, 9), line_of(b), :]

        return Ring(where, whole, half, ring_send.at[c], ring_recv.at[c])

    near, rest = right_ring(0), right_ring(1)
    near.start()
    rest.start()

    own_copies[1].wait()
    for n, (dy, dz) in enumerate(YZ_OFFSETS):
        from_yz = wrap(y - dy, NY) * NZ + wrap(z - dz, NZ)
        remote(l_send.at[0], l_all.at[x, from_yz], yz_send.at[n], yz_recv.at[n], me).wait_recv()
    for n in range(3):
        go(over_x(0, n, l_all.at[x], l_all.at[x]))
    send_qkv(0)

    near.step(1)
    rest.step(1)

    w_outer_wide[...] = w_outer[...].astype(F32)
    for k in range(8):
        w_outer_t[:, 128 * k : 128 * k + 128] = (
            jnp.concatenate([w_outer_wide[pl.ds(4 * k + t, 32, stride=32), :] for t in range(4)], axis=0)
            .T.astype(BF16)
        )

    near.step(2)
    rest.step(2)

    for n in range(3):
        over_x(0, n, l_all.at[x], l_all.at[from_x(n)]).wait_recv()
    l_wide[...] = l_all[...].astype(F32).reshape(2048, 128)
    for pair in range(16):
        block = jnp.concatenate(
            [l_wide[pl.ds(2 * pair, 64, stride=32), :], l_wide[pl.ds(2 * pair + 1, 64, stride=32), :]],
            axis=0,
        ).T
        for e in range(2):
            l_mixed[pl.ds((2 * pair + e) * 32, 32), :] = jnp.concatenate(
                [block[32 * s : 32 * s + 32, 64 * e : 64 * e + 64] for s in range(4)], axis=1
            ).astype(BF16)
    source = lax.broadcasted_iota(jnp.int32, (256, 256), 0)
    target = lax.broadcasted_iota(jnp.int32, (256, 256), 1)
    place = lax.rem(source, 16) * 16 + lax.rem(lax.div(source, 16), 4) * 4 + lax.div(source, 64)
    order = jnp.where(place == target, 1.0, 0.0).astype(BF16)
    l_t[...] = jnp.dot(l_mixed[...], order, preferred_element_type=F32).astype(BF16)

    own_copies[2].wait()
    for n in range(3):
        over_x(1, n, cpl.at[:, pl.ds(0, 128), :], couple.at[from_x(n)]).wait_recv()

    def turn_couple(g, carry):
        for i in range(8):
            couple_t[g, i] = couple[g, i].astype(F32).T
        return carry

    lax.fori_loop(0, 4, turn_couple, 0)
    near.step(3)
    send_qkv(1, (0,))
    rest.step(3)
    near.finish()

    def outer_rows(g, first, last):
        l_rows = l_t[pl.ds(pl.multiple_of(g * 256, 256), 256), :]
        for d in range(first, last):
            right = jnp.concatenate([r_all[2 * d], r_all[2 * d + 1]], axis=1)
            product = jnp.dot(l_rows, right, preferred_element_type=F32).astype(BF16)
            for e in range(2):
                outer[pl.ds(8 * g, 8), (2 * d + e) * 32 : (2 * d + e) * 32 + 32, :] = product[
                    :, 128 * e : 128 * e + 128
                ].reshape(8, 32, 128)

    def outer_near(g, carry):
        outer_rows(g, 0, 9)
        return carry

    lax.fori_loop(0, 4, outer_near, 0)
    rest.finish()

    plane = r_all[32 + lax.div(y, 2)].astype(F32).T.astype(BF16)
    together = jnp.dot(plane, r_all[32 + x], preferred_element_type=F32).astype(BF16)
    row = lax.broadcasted_iota(jnp.int32, (32, 128), 0)
    column = lax.broadcasted_iota(jnp.int32, (32, 128), 1)
    chosen = 64 * lax.rem(y, 2) + 16 * lax.div(row, 8) + 8 * z + lax.rem(row, 8)
    pick = jnp.where(chosen == column, 1.0, 0.0).astype(BF16)
    counts[...] = 1.0 / (jnp.dot(pick, together, preferred_element_type=F32) + 0.001)

    w_bias = jnp.concatenate([w_bias_t[...]] * 3, axis=1)

    def outer_rest(g, carry):
        outer_rows(g, 9, 16)
        offsets = []
        for pair in range(4):
            right = jnp.concatenate([outer[8 * g + 2 * pair], outer[8 * g + 2 * pair + 1]], axis=1)
            update = jnp.dot(w_outer_t[...], right, preferred_element_type=F32)
            standards = []
            for e in range(2):
                i = 2 * pair + e
                scaled = update[:, 128 * e : 128 * e + 128] * counts[pl.ds(g * 8 + i, 1), :]
                updated = (couple_t[g, i] + scaled).astype(BF16)
                updated_t[g, i] = updated
                updated = updated.astype(F32)
                mean = jnp.mean(updated, axis=0, keepdims=True)
                centered = updated - mean
                variance = jnp.mean(centered * centered, axis=0, keepdims=True)
                standards.append(centered * lax.rsqrt(variance + 1e-05))
            standard = jnp.concatenate(standards, axis=1)
            part_a = standard.astype(BF16)
            left_over = standard - part_a.astype(F32)
            part_b = left_over.astype(BF16)
            part_c = (left_over - part_b.astype(F32)).astype(BF16)
            both = (
                jnp.dot(
                    w_bias, jnp.concatenate([part_a, part_b, part_c], axis=0), preferred_element_type=F32
                )
                * LOG2E
            )
            offsets += [both[:, :128], both[:, 128:]]
        for h in range(8):
            bias_block[h, g] = jnp.concatenate([v[h : h + 1] for v in offsets], axis=0)
        return carry

    def send_bias(c):
        half_rows = pl.ds(2 * c, 2)
        for h in range(2):
            for n in range(7):
                go(
                    over_xz(
                        1 + 2 * c + h,
                        n,
                        bias_block.at[2 * to_xz(n) + h, half_rows],
                        bias.at[h, y, half_rows, z, :, block_of(x)],
                    )
                )
        copy = pltpu.make_async_copy(
            bias_block.at[pl.ds(2 * x, 2), half_rows],
            bias.at[:, y, half_rows, z, :, block_of(x)],
            own.at[(4, 8)[c]],
        )
        copy.start()
        return copy

    lax.fori_loop(0, 2, outer_rest, 0)
    own_bias = [send_bias(0)]
    lax.fori_loop(2, 4, outer_rest, 0)
    own_bias.append(send_bias(1))

    present = jnp.concatenate([r_all[32 + k, pl.ds(pl.multiple_of(16 * yz, 16), 16), :] for k in range(4)], axis=1).astype(F32) - 1.0
    penalty[...] = jnp.concatenate(
        [present * PENALTY[0], present * PENALTY[1], present * PENALTY[2], jnp.zeros((80, 512), F32)],
        axis=0,
    ).astype(BF16)

    def arrive_bias(c):
        half_rows = pl.ds(2 * c, 2)
        own_bias[c].wait()
        for h in range(2):
            for n in range(7):
                other_x, other_z = from_xz(n)
                over_xz(
                    1 + 2 * c + h,
                    n,
                    bias_block.at[0, half_rows],
                    bias.at[h, y, half_rows, other_z, :, block_of(other_x)],
                ).wait_recv()

    def bias_ring(h, c):
        def whole(b):
            return bias.at[h, b, pl.ds(2 * c, 2)]

        def half(b, way):
            return bias.at[h, b, 2 * c + way]

        number = 2 + 2 * h + c
        return Ring(where, whole, half, ring_send.at[number], ring_recv.at[number])

    r0, r1, r2, r3 = [bias_ring(h, c) for h in range(2) for c in range(2)]
    arrive_bias(0)
    r0.start()
    r2.start()
    arrive_bias(1)
    r1.start()
    r3.start()
    send_qkv(1, (1, 2))

    def attend(h, owner, blocks):
        count = 64 * len(blocks)
        lane = lax.broadcasted_iota(jnp.int32, (count, 128), 1)
        offset = jnp.concatenate([bias[h, b].reshape(64, 512) for b in blocks], axis=0)
        query = jnp.concatenate([qv[owner, h, 0, b].reshape(64, 128) for b in blocks], axis=0)
        every = qv[owner, h, 1].reshape(512, 128)
        weights, values = [], []
        for e in range(4):
            inside = groups == e
            keys = [jnp.zeros((32, 512), BF16)] * 4
            keys[e] = k_got[owner, h, 32 * e : 32 * e + 32, :]
            key = jnp.concatenate(keys + [penalty[...]], axis=0)
            value = jnp.where(inside, every, jnp.zeros((), BF16))
            values.append(jnp.concatenate([value, jnp.where(inside, 1.0, 0.0).astype(BF16)], axis=1))
            marked = (lax.rem(lane, 16) == owner * 4 + e) & (lane < 48)
            left = jnp.concatenate([query, jnp.where(marked, 1.0, 0.0).astype(BF16)], axis=1)
            scores = jnp.dot(left, key, preferred_element_type=F32) * SCORE_SCALE + offset
            top = jnp.max(scores, axis=-1, keepdims=True)
            weights.append(jnp.exp2(scores - top).astype(BF16))
        both = jnp.dot(
            jnp.concatenate(weights, axis=1),
            jnp.concatenate(values, axis=0),
            preferred_element_type=F32,
        )
        result = (both[:, :128] / both[:, 128:]).astype(BF16).reshape(len(blocks), 4, 16, 128)
        for k, b in enumerate(blocks):
            att_send[owner, h, b] = result[k]

    def back(h, n, o):
        b = wrap(y + o, NY)
        return remote(
            att_send.at[to_x(n), h, b],
            att.at[x, h, b],
            att_out.at[h, n, o % NY],
            att_in.at[h, n, o % NY],
            index_of(y, to_x(n), z),
        )

    def run(h, offsets):
        blocks = [wrap(y + o, NY) for o in offsets]

        def body(k, carry):
            shift = jnp.where(k == 0, 2, jnp.where(k == 1, 1, jnp.where(k == 2, 3, 0)))
            attend(h, wrap(x + shift, NX), blocks)
            for slot, n in enumerate((2, 0, 1)):
                pl.when(k == slot)(lambda n=n: perform([back(h, n, o).start for o in offsets]))
            return carry

        lax.fori_loop(0, 4, body, 0)

    def turn_updated(g, carry):
        for i in range(8):
            pair_send[g, i] = updated_t[g, i].astype(F32).T.astype(BF16)
        return carry

    for copy in own_qkv:
        copy.wait()
    for n in range(3):
        arrive_qkv(0, n)
    run(0, (0,))
    r0.step(1)
    r1.step(1)
    lax.fori_loop(0, 4, turn_updated, 0)
    for n in range(3):
        go(over_x(2, n, pair_send.at[to_x(n)], out_pair.at[:, block_of(x), :]))
    own_pair = pltpu.make_async_copy(pair_send.at[x], out_pair.at[:, block_of(x), :], own.at[5])
    own_pair.start()
    r2.step(1)
    r3.step(1)
    run(0, (1, -1))
    r0.step(2)
    r1.step(2)
    r2.step(2)
    r3.step(2)
    run(0, (2, -2))
    r0.step(3)
    r1.step(3)
    for n in range(3):
        arrive_qkv(1, n)
    run(1, (0, 1, -1))
    r2.step(3)
    r3.step(3)
    run(1, (2, -2))
    r0.finish()
    r1.finish()
    run(0, (3, -3, 4))
    r2.finish()
    r3.finish()
    run(1, (3, -3, 4))
    own_att = pltpu.make_async_copy(att_send.at[x], att.at[x], own.at[6])
    own_att.start()
    own_att.wait()
    for h in range(2):
        for n in (2, 0, 1):
            for o in range(NY):
                b = wrap(y + o, NY)
                remote(
                    att_send.at[0, h, b], att.at[from_x(n), h, b], att_out.at[h, n, o], att_in.at[h, n, o], me
                ).wait_recv()
        for k in range(NX):
            out_gated[2 * k + h] = (att[k, h].reshape(512, 128).astype(F32) * gate[k, h]).astype(BF16)

    own_pair.wait()
    for n in range(3):
        over_x(2, n, pair_send.at[0], out_pair.at[:, block_of(from_x(n)), :]).wait_recv()
    for h in range(2):
        for n in range(3):
            for o in range(NY):
                back(h, n, o).wait_send()
    for copy in sent:
        copy.wait_send()
    for one in (near, rest, r0, r1, r2, r3):
        one.drain()


def finish(gated, hom, pair, w_final, out_hom, out_pair):
    out_pair[...] = pair[...]
    quads = [regroup(*[gated[4 * b + t].astype(F32) for t in range(4)]) for b in range(2)]
    joined = jnp.concatenate(
        [jnp.concatenate([quads[0][s], quads[1][s]], axis=1).astype(BF16) for s in range(4)], axis=0
    )
    update = jnp.dot(joined, w_final[...], preferred_element_type=F32)
    out_hom[...] = (hom[...].astype(F32) + update.reshape(4, 128, 256)).astype(BF16)


def on_device(
    homolog_tensor,
    couple_tensor,
    homolog_presence,
    asking_matrix,
    lookup_matrix,
    content_matrix,
    sigmoid_matrix,
    sigmoid_offset,
    attention_final_matrix,
    first_factor_matrix,
    second_factor_matrix,
    tensor_product_matrix,
    couple_offset_matrix,
):
    vmem = pl.BlockSpec(memory_space=pltpu.VMEM)
    dma = pltpu.SemaphoreType.DMA
    scratch = [
        pltpu.VMEM((4, 512, 256), BF16),
        pltpu.VMEM((16, 32, 128), BF16),
        pltpu.VMEM((4, 16, 32, 128), BF16),
        pltpu.VMEM((4, 4, ROWS, 128), BF16),
        pltpu.VMEM((2, 4, 4, ROWS, 128), BF16),
        pltpu.VMEM((32 * ROWS, 128), F32),
        pltpu.VMEM((PLANES, 256, 128), BF16),
        pltpu.VMEM((2048, 128), F32),
        pltpu.VMEM((1024, 256), BF16),
        pltpu.VMEM((1024, 256), BF16),
        pltpu.VMEM((1024, 128), F32),
        pltpu.VMEM((128, 1024), BF16),
        pltpu.VMEM((4, 2, 2, 8, 4, 16, 128), BF16),
        pltpu.VMEM((4, 2, 2, 8, 4, 16, 128), BF16),
        pltpu.VMEM((4, 2, 128, 512), BF16),
        pltpu.VMEM((4, 2, 128, 512), BF16),
        pltpu.VMEM((4, 2, 512, 128), F32),
        pltpu.VMEM((4, 8, 128, 128), BF16),
        pltpu.VMEM((4, 8, 128, 128), F32),
        pltpu.VMEM((4, 8, 128, 128), BF16),
        pltpu.VMEM((32, 128), F32),
        pltpu.VMEM((32, 1024, 128), BF16),
        pltpu.VMEM((4, 8, 128, 128), BF16),
        pltpu.VMEM((8, 4, 8, 128), F32),
        pltpu.VMEM((2, 8, 4, 2, 8, 512), F32),
        pltpu.VMEM((128, 512), BF16),
        pltpu.VMEM((4, 2, 8, 4, 16, 128), BF16),
        pltpu.VMEM((4, 2, 8, 4, 16, 128), BF16),
        dma((11, 3)),
        dma((11, 3)),
        dma((5, 7)),
        dma((5, 7)),
        dma((15,)),
        dma((15,)),
        dma((6, 2, 4)),
        dma((6, 2, 4)),
        dma((2, 3, 8)),
        dma((2, 3, 8)),
        dma((9,)),
    ]
    gated, pair = pl.pallas_call(
        kernel,
        name="evoformer_block",
        out_shape=(
            jax.ShapeDtypeStruct((8, 512, 128), BF16),
            jax.ShapeDtypeStruct((8, 512, 128), BF16),
        ),
        in_specs=[vmem] * 12,
        out_specs=(vmem, vmem),
        scratch_shapes=scratch,
        compiler_params=pltpu.CompilerParams(
            collective_id=1, has_side_effects=True, vmem_limit_bytes=60 << 20
        ),
    )(
        homolog_tensor,
        couple_tensor,
        homolog_presence,
        asking_matrix,
        lookup_matrix,
        content_matrix,
        sigmoid_matrix,
        sigmoid_offset,
        first_factor_matrix.T,
        second_factor_matrix.T,
        tensor_product_matrix,
        couple_offset_matrix.T,
    )
    rows = lambda lead, width: pl.BlockSpec((lead, 128, width), lambda i: (0, i, 0))
    return pl.pallas_call(
        finish,
        name="final_projection",
        grid=(4,),
        out_shape=(
            jax.ShapeDtypeStruct((4, 512, 256), BF16),
            jax.ShapeDtypeStruct((8, 512, 128), BF16),
        ),
        in_specs=[
            rows(8, 128),
            rows(4, 256),
            rows(8, 128),
            pl.BlockSpec((256, 256), lambda i: (0, 0)),
        ],
        out_specs=(rows(4, 256), rows(8, 128)),
    )(gated, homolog_tensor, pair, attention_final_matrix)


def solution(mesh):
    return jax.shard_map(
        on_device,
        mesh=mesh,
        in_specs=(
            P(("dp", "dap"), None, None),
            P(("dp", "dap"), None, None),
            P(("dp", "dap"), None),
            P(),
            P(),
            P(),
            P(),
            P(),
            P(),
            P(),
            P(),
            P(),
            P(),
        ),
        out_specs=(P(("dp", "dap"), None, None), P(("dp", "dap"), None, None)),
        check_vma=False,
    )
```

```python
import functools
import math

import jax
import jax.numpy as jnp
from jax import lax
from jax.experimental import pallas as pl
from jax.experimental.pallas import tpu as pltpu
from jax.sharding import PartitionSpec as P

MESH = pl.DeviceIdType.MESH
F32 = jnp.float32
BF16 = jnp.bfloat16
LOG2E = math.log2(math.e)
SCORE_SCALE = 32.0**-0.5 * LOG2E
PENALTY = (56576.0, -7.46875, 0.01123046875)

NY, NX, NZ = 8, 4, 2
PLANES = 36
ROWS = 48
YZ_OFFSETS = [(dy, dz) for dz in range(NZ) for dy in range(NY) if (dy, dz) != (0, 0)]
X_OFFSETS = (1, 3, 2)
XZ_OFFSETS = [(dx, dz) for dx in (1, 3, 2, 0) for dz in range(NZ) if (dx, dz) != (0, 0)]


def wrap(value, size):
    return lax.rem(value + size, size)


def index_of(y, x, z):
    return (y * NX + x) * NZ + z


def remote(src, dst, send, recv, device):
    return pltpu.make_async_remote_copy(
        src_ref=src,
        dst_ref=dst,
        send_sem=send,
        recv_sem=recv,
        device_id={"dap": device},
        device_id_type=MESH,
    )


class Ring:
    def __init__(self, where, whole, half, send, recv):
        self.y, self.x, self.z = where
        self.whole, self.half = whole, half
        self.send, self.recv = send, recv

    def copy(self, way, step, block):
        view = self.half(block, way) if step == 3 else self.whole(block)
        to = wrap(self.y + (1 if way == 0 else -1), NY)
        return remote(
            view, view, self.send.at[way, step], self.recv.at[way, step], index_of(to, self.x, self.z)
        )

    def start(self):
        for way in (0, 1):
            self.copy(way, 0, self.y).start()

    def step(self, number):
        for way in (0, 1):
            block = wrap(self.y + (-number if way == 0 else number), NY)
            self.copy(way, number - 1, block).wait_recv()
            self.copy(way, number, block).start()

    def finish(self):
        for way in (0, 1):
            self.copy(way, 3, wrap(self.y + 4, NY)).wait_recv()

    def drain(self):
        for way in (0, 1):
            for step in range(4):
                self.copy(way, step, self.y).wait_send()


def regroup(v0, v1, v2, v3):
    lane = lax.broadcasted_iota(jnp.int32, v0.shape, 1)
    low = lane < 64
    even = lax.rem(lax.div(lane, 32), 2) == 0
    u0 = jnp.where(low, v0, pltpu.roll(v2, 64, 1))
    u2 = jnp.where(low, pltpu.roll(v0, 64, 1), v2)
    u1 = jnp.where(low, v1, pltpu.roll(v3, 64, 1))
    u3 = jnp.where(low, pltpu.roll(v1, 64, 1), v3)
    return (
        jnp.where(even, u0, pltpu.roll(u1, 32, 1)),
        jnp.where(even, pltpu.roll(u0, 96, 1), u1),
        jnp.where(even, u2, pltpu.roll(u3, 32, 1)),
        jnp.where(even, pltpu.roll(u2, 96, 1), u3),
    )


def perform(actions):
    for action in actions:
        action()


def normalize_rows(values):
    mean = jnp.mean(values, axis=-1, keepdims=True)
    centered = values - mean
    variance = jnp.mean(centered * centered, axis=-1, keepdims=True)
    return centered * lax.rsqrt(variance + 1e-05)


def nt_dot(left, right):
    return lax.dot_general(left, right, (((1,), (1,)), ((), ())), preferred_element_type=F32)


def kernel(
    hom,
    cpl,
    presence,
    w_query,
    w_key,
    w_value,
    w_gate,
    gate_offset,
    w_left_t,
    w_right_t,
    w_outer,
    w_bias_t,
    out_gated,
    out_pair,
    normed,
    l_send,
    l_all,
    r_send,
    r_got,
    r_wide,
    r_all,
    l_wide,
    l_mixed,
    l_t,
    w_outer_wide,
    w_outer_t,
    qv_send,
    qv,
    k_send,
    k_got,
    gate,
    couple,
    couple_t,
    updated_t,
    counts,
    outer,
    pair_send,
    bias_block,
    bias,
    penalty,
    att_send,
    att,
    x_send,
    x_recv,
    xz_send,
    xz_recv,
    yz_send,
    yz_recv,
    ring_send,
    ring_recv,
    own,
):
    me = lax.axis_index("dap")
    y = lax.div(me, NX * NZ)
    x = lax.rem(lax.div(me, NZ), NX)
    z = lax.rem(me, NZ)
    yz = y * NZ + z
    where = (y, x, z)

    barrier = pltpu.get_barrier_semaphore()
    for dx, dz in XZ_OFFSETS:
        if dx != 0:
            pl.semaphore_signal(
                barrier,
                inc=1,
                device_id={"dap": index_of(y, wrap(x + dx, NX), wrap(z + dz, NZ))},
                device_id_type=MESH,
            )
    for dy, dz in YZ_OFFSETS:
        pl.semaphore_signal(
            barrier,
            inc=1,
            device_id={"dap": index_of(wrap(y + dy, NY), x, wrap(z + dz, NZ))},
            device_id_type=MESH,
        )

    def over_x(kind, n, src, dst):
        to = index_of(y, wrap(x + X_OFFSETS[n], NX), z)
        return remote(src, dst, x_send.at[kind, n], x_recv.at[kind, n], to)

    def over_xz(kind, n, src, dst):
        dx, dz = XZ_OFFSETS[n]
        to = index_of(y, wrap(x + dx, NX), wrap(z + dz, NZ))
        return remote(src, dst, xz_send.at[kind, n], xz_recv.at[kind, n], to)

    def to_xz(n):
        return wrap(x + XZ_OFFSETS[n][0], NX)

    def from_xz(n):
        dx, dz = XZ_OFFSETS[n]
        return wrap(x - dx, NX), wrap(z - dz, NZ)

    def to_x(n):
        return wrap(x + X_OFFSETS[n], NX)

    def from_x(n):
        return wrap(x - X_OFFSETS[n], NX)

    sent = []

    def go(copy):
        copy.start()
        sent.append(copy)

    def block_of(k):
        return pl.ds(pl.multiple_of(128 * k, 128), 128)

    lanes = lax.broadcasted_iota(jnp.int32, (512, 128), 1)
    groups = lax.div(lanes, 32)

    def project_right(s, carry):
        lines = normalize_rows(hom[s].astype(F32)).astype(BF16)
        normed[s] = lines
        present = presence[pl.ds(s, 1), :].astype(F32)
        right = (nt_dot(w_right_t[...], lines) * present).astype(BF16)
        rows = jnp.concatenate(
            [present[:, 128 * k : 128 * k + 128] for k in range(4)] + [jnp.zeros((12, 128), F32)], axis=0
        ).astype(BF16)
        for k in range(NX):
            r_send[k, s, 0:32, :] = right[:, 128 * k : 128 * k + 128]
            r_send[k, s, 32:48, :] = rows
        return carry

    lax.fori_loop(0, 4, project_right, 0)
    pl.semaphore_wait(barrier, 6 + len(YZ_OFFSETS))
    for n in range(7):
        go(over_xz(0, n, r_send.at[to_xz(n)], r_got.at[z, x]))

    w_left = jnp.concatenate([w_left_t[...]] * 4, axis=0)

    def project_left(s, total):
        return jnp.where(groups == s, nt_dot(normed[s], w_left), total)

    left = lax.fori_loop(0, 4, project_left, jnp.zeros((512, 128), F32))
    spread = jnp.where(
        lax.div(lax.broadcasted_iota(jnp.int32, (128, 128), 1), 32)
        == lax.broadcasted_iota(jnp.int32, (128, 128), 0),
        1.0,
        0.0,
    ).astype(BF16)
    tall = jnp.concatenate([presence[...].astype(F32), jnp.zeros((124, 512), F32)], axis=0).T
    left = left * jnp.dot(tall.astype(BF16), spread, preferred_element_type=F32)
    left = left.reshape(NY, NX, NZ, 8, 128)
    for b in range(NY):
        for c in range(NZ):
            l_send[b * NZ + c] = left[b, :, c].reshape(32, 128).astype(BF16)

    for n, (dy, dz) in enumerate(YZ_OFFSETS):
        to_y, to_z = wrap(y + dy, NY), wrap(z + dz, NZ)
        go(
            remote(
                l_send.at[to_y * NZ + to_z],
                l_all.at[x, yz],
                yz_send.at[n],
                yz_recv.at[n],
                index_of(to_y, x, to_z),
            )
        )
    for n in range(3):
        go(over_x(1, n, cpl.at[:, block_of(to_x(n)), :], couple.at[x]))
    own_copies = [
        pltpu.make_async_copy(r_send.at[x], r_got.at[z, x], own.at[0]),
        pltpu.make_async_copy(l_send.at[yz], l_all.at[x, yz], own.at[1]),
        pltpu.make_async_copy(cpl.at[:, block_of(x), :], couple.at[x], own.at[2]),
    ]
    for copy in own_copies:
        copy.start()

    def heads(part, carry):
        rows = pl.ds(pl.multiple_of(128 * part, 128), 128)
        for kind, w in enumerate((w_query, w_value, w_gate)):
            made = [jnp.dot(normed[s, rows, :], w[...], preferred_element_type=F32) for s in range(4)]
            if kind == 2:
                made = [jax.nn.sigmoid(m + offset_row) for m in made]
            for b in range(2):
                outs = regroup(*[m[:, 128 * b : 128 * b + 128] for m in made])
                for t in range(4):
                    h = 4 * b + t
                    if kind == 2:
                        gate[h // 2, h % 2, rows, :] = outs[t]
                    else:
                        qv_send[h // 2, h % 2, kind, pl.ds(2 * part, 2)] = (
                            outs[t].astype(BF16).reshape(2, 4, 16, 128)
                        )
        return carry

    offset_row = gate_offset[...].astype(F32).reshape(1, 256)
    w_key_t = w_key[...].astype(F32).T.astype(BF16)

    def keys(s, carry):
        made = nt_dot(w_key_t, normed[s]).astype(BF16)
        for h in range(8):
            k_send[h // 2, h % 2, pl.ds(pl.multiple_of(32 * s, 32), 32), :] = made[32 * h : 32 * h + 32]
        return carry


    def qkv_copies(h, n):
        other = from_x(n)
        return (
            (5 + 3 * h, k_send.at[to_x(n), h], k_got.at[x, h], k_got.at[other, h]),
            (6 + 3 * h, qv_send.at[to_x(n), h, 1], qv.at[x, h, 1], qv.at[other, h, 1]),
            (7 + 3 * h, qv_send.at[to_x(n), h, 0], qv.at[x, h, 0], qv.at[other, h, 0]),
        )

    def send_qkv(h, kinds=(0, 1, 2)):
        for k in kinds:
            for n in range(3):
                kind, src, dst, _ = qkv_copies(h, n)[k]
                go(over_x(kind, n, src, dst))

    def arrive_qkv(h, n):
        for kind, src, _, got in qkv_copies(h, n):
            over_x(kind, n, src, got).wait_recv()

    own_qkv = [
        pltpu.make_async_copy(k_send.at[x], k_got.at[x], own.at[3]),
        pltpu.make_async_copy(qv_send.at[x], qv.at[x], own.at[7]),
    ]
    own_copies[0].wait()
    for n in range(7):
        other_x, other_z = from_xz(n)
        over_xz(0, n, r_send.at[0], r_got.at[other_z, other_x]).wait_recv()
    r_wide[...] = r_got[...].astype(F32).reshape(32 * ROWS, 128)

    def line_of(b):
        return pl.ds(pl.multiple_of(32 * b, 32), 32)

    for q in range(PLANES):
        r_all[q, line_of(y), :] = r_wide[pl.ds(q, 32, stride=ROWS), :].astype(BF16)

    def right_ring(c):
        first = (0, 18)[c]

        def whole(b):
            return r_all.at[pl.ds(first, 18), line_of(b), :]

        def half(b, way):
            return r_all.at[pl.ds(first + 9 * way, 9), line_of(b), :]

        return Ring(where, whole, half, ring_send.at[c], ring_recv.at[c])

    near, rest = right_ring(0), right_ring(1)
    near.start()
    rest.start()

    own_copies[1].wait()
    for n, (dy, dz) in enumerate(YZ_OFFSETS):
        from_yz = wrap(y - dy, NY) * NZ + wrap(z - dz, NZ)
        remote(l_send.at[0], l_all.at[x, from_yz], yz_send.at[n], yz_recv.at[n], me).wait_recv()
    for n in range(3):
        go(over_x(0, n, l_all.at[x], l_all.at[x]))
    lax.fori_loop(0, 4, keys, 0)
    lax.fori_loop(0, 4, heads, 0)
    for copy in own_qkv:
        copy.start()
    send_qkv(0)

    near.step(1)
    rest.step(1)

    w_outer_wide[...] = w_outer[...].astype(F32)
    for k in range(8):
        w_outer_t[:, 128 * k : 128 * k + 128] = (
            jnp.concatenate([w_outer_wide[pl.ds(4 * k + t, 32, stride=32), :] for t in range(4)], axis=0)
            .T.astype(BF16)
        )

    near.step(2)
    rest.step(2)

    for n in range(3):
        over_x(0, n, l_all.at[x], l_all.at[from_x(n)]).wait_recv()
    l_wide[...] = l_all[...].astype(F32).reshape(2048, 128)
    for pair in range(16):
        block = jnp.concatenate(
            [l_wide[pl.ds(2 * pair, 64, stride=32), :], l_wide[pl.ds(2 * pair + 1, 64, stride=32), :]],
            axis=0,
        ).T
        for e in range(2):
            l_mixed[pl.ds((2 * pair + e) * 32, 32), :] = jnp.concatenate(
                [block[32 * s : 32 * s + 32, 64 * e : 64 * e + 64] for s in range(4)], axis=1
            ).astype(BF16)
    source = lax.broadcasted_iota(jnp.int32, (256, 256), 0)
    target = lax.broadcasted_iota(jnp.int32, (256, 256), 1)
    place = lax.rem(source, 16) * 16 + lax.rem(lax.div(source, 16), 4) * 4 + lax.div(source, 64)
    order = jnp.where(place == target, 1.0, 0.0).astype(BF16)
    l_t[...] = jnp.dot(l_mixed[...], order, preferred_element_type=F32).astype(BF16)

    own_copies[2].wait()
    for n in range(3):
        over_x(1, n, cpl.at[:, pl.ds(0, 128), :], couple.at[from_x(n)]).wait_recv()

    def turn_couple(g, carry):
        for i in range(8):
            couple_t[g, i] = couple[g, i].astype(F32).T
        return carry

    lax.fori_loop(0, 4, turn_couple, 0)
    near.step(3)
    send_qkv(1, (0, 1))
    rest.step(3)
    near.finish()

    def outer_rows(g, first, last):
        l_rows = l_t[pl.ds(pl.multiple_of(g * 256, 256), 256), :]
        for d in range(first, last):
            right = jnp.concatenate([r_all[2 * d], r_all[2 * d + 1]], axis=1)
            product = jnp.dot(l_rows, right, preferred_element_type=F32).astype(BF16)
            for e in range(2):
                outer[pl.ds(8 * g, 8), (2 * d + e) * 32 : (2 * d + e) * 32 + 32, :] = product[
                    :, 128 * e : 128 * e + 128
                ].reshape(8, 32, 128)

    def outer_near(g, carry):
        outer_rows(g, 0, 9)
        return carry

    lax.fori_loop(0, 4, outer_near, 0)
    rest.finish()

    plane = r_all[32 + lax.div(y, 2)].astype(F32).T.astype(BF16)
    together = jnp.dot(plane, r_all[32 + x], preferred_element_type=F32).astype(BF16)
    row = lax.broadcasted_iota(jnp.int32, (32, 128), 0)
    column = lax.broadcasted_iota(jnp.int32, (32, 128), 1)
    chosen = 64 * lax.rem(y, 2) + 16 * lax.div(row, 8) + 8 * z + lax.rem(row, 8)
    pick = jnp.where(chosen == column, 1.0, 0.0).astype(BF16)
    counts[...] = 1.0 / (jnp.dot(pick, together, preferred_element_type=F32) + 0.001)

    w_bias = jnp.concatenate([w_bias_t[...]] * 3, axis=1)

    def outer_rest(g, carry):
        outer_rows(g, 9, 16)
        offsets = []
        for pair in range(4):
            right = jnp.concatenate([outer[8 * g + 2 * pair], outer[8 * g + 2 * pair + 1]], axis=1)
            update = jnp.dot(w_outer_t[...], right, preferred_element_type=F32)
            standards = []
            for e in range(2):
                i = 2 * pair + e
                scaled = update[:, 128 * e : 128 * e + 128] * counts[pl.ds(g * 8 + i, 1), :]
                updated = (couple_t[g, i] + scaled).astype(BF16)
                updated_t[g, i] = updated
                updated = updated.astype(F32)
                mean = jnp.mean(updated, axis=0, keepdims=True)
                centered = updated - mean
                variance = jnp.mean(centered * centered, axis=0, keepdims=True)
                standards.append(centered * lax.rsqrt(variance + 1e-05))
            standard = jnp.concatenate(standards, axis=1)
            part_a = standard.astype(BF16)
            left_over = standard - part_a.astype(F32)
            part_b = left_over.astype(BF16)
            part_c = (left_over - part_b.astype(F32)).astype(BF16)
            both = (
                jnp.dot(
                    w_bias, jnp.concatenate([part_a, part_b, part_c], axis=0), preferred_element_type=F32
                )
                * LOG2E
            )
            offsets += [both[:, :128], both[:, 128:]]
        for h in range(8):
            bias_block[h, g] = jnp.concatenate([v[h : h + 1] for v in offsets], axis=0)
        return carry

    def send_bias(c):
        half_rows = pl.ds(2 * c, 2)
        for h in range(2):
            for n in range(7):
                go(
                    over_xz(
                        1 + 2 * c + h,
                        n,
                        bias_block.at[2 * to_xz(n) + h, half_rows],
                        bias.at[h, y, half_rows, z, :, block_of(x)],
                    )
                )
        copy = pltpu.make_async_copy(
            bias_block.at[pl.ds(2 * x, 2), half_rows],
            bias.at[:, y, half_rows, z, :, block_of(x)],
            own.at[(4, 8)[c]],
        )
        copy.start()
        return copy

    lax.fori_loop(0, 2, outer_rest, 0)
    own_bias = [send_bias(0)]
    lax.fori_loop(2, 4, outer_rest, 0)
    own_bias.append(send_bias(1))

    present = jnp.concatenate([r_all[32 + k, pl.ds(pl.multiple_of(16 * yz, 16), 16), :] for k in range(4)], axis=1).astype(F32) - 1.0
    penalty[...] = jnp.concatenate(
        [present * PENALTY[0], present * PENALTY[1], present * PENALTY[2], jnp.zeros((80, 512), F32)],
        axis=0,
    ).astype(BF16)

    def arrive_bias(c):
        half_rows = pl.ds(2 * c, 2)
        own_bias[c].wait()
        for h in range(2):
            for n in range(7):
                other_x, other_z = from_xz(n)
                over_xz(
                    1 + 2 * c + h,
                    n,
                    bias_block.at[0, half_rows],
                    bias.at[h, y, half_rows, other_z, :, block_of(other_x)],
                ).wait_recv()

    def bias_ring(h, c):
        def whole(b):
            return bias.at[h, b, pl.ds(2 * c, 2)]

        def half(b, way):
            return bias.at[h, b, 2 * c + way]

        number = 2 + 2 * h + c
        return Ring(where, whole, half, ring_send.at[number], ring_recv.at[number])

    r0, r1, r2, r3 = [bias_ring(h, c) for h in range(2) for c in range(2)]
    arrive_bias(0)
    r0.start()
    r2.start()
    arrive_bias(1)
    r1.start()
    r3.start()
    send_qkv(1, (2,))

    def attend(h, owner, blocks):
        count = 64 * len(blocks)
        lane = lax.broadcasted_iota(jnp.int32, (count, 128), 1)
        offset = jnp.concatenate([bias[h, b].reshape(64, 512) for b in blocks], axis=0)
        query = jnp.concatenate([qv[owner, h, 0, b].reshape(64, 128) for b in blocks], axis=0)
        every = qv[owner, h, 1].reshape(512, 128)
        weights, values = [], []
        for e in range(4):
            inside = groups == e
            keys = [jnp.zeros((32, 512), BF16)] * 4
            keys[e] = k_got[owner, h, 32 * e : 32 * e + 32, :]
            key = jnp.concatenate(keys + [penalty[...]], axis=0)
            value = jnp.where(inside, every, jnp.zeros((), BF16))
            values.append(jnp.concatenate([value, jnp.where(inside, 1.0, 0.0).astype(BF16)], axis=1))
            marked = (lax.rem(lane, 16) == owner * 4 + e) & (lane < 48)
            left = jnp.concatenate([query, jnp.where(marked, 1.0, 0.0).astype(BF16)], axis=1)
            scores = jnp.dot(left, key, preferred_element_type=F32) * SCORE_SCALE + offset
            top = jnp.max(scores, axis=-1, keepdims=True)
            weights.append(jnp.exp2(scores - top).astype(BF16))
        both = jnp.dot(
            jnp.concatenate(weights, axis=1),
            jnp.concatenate(values, axis=0),
            preferred_element_type=F32,
        )
        result = (both[:, :128] / both[:, 128:]).astype(BF16).reshape(len(blocks), 4, 16, 128)
        for k, b in enumerate(blocks):
            att_send[owner, h, b] = result[k]

    def run(h, offsets, after=()):
        blocks = [wrap(y + o, NY) for o in offsets]

        def body(n, carry):
            shift = jnp.where(n == 0, 2, jnp.where(n == 1, 1, jnp.where(n == 2, 3, 0)))
            attend(h, wrap(x + shift, NX), blocks)
            for k, action in enumerate(after):
                pl.when(n == k)(action)
            return carry

        lax.fori_loop(0, 4, body, 0)

    def turn_updated(g, carry):
        for i in range(8):
            pair_send[g, i] = updated_t[g, i].astype(F32).T.astype(BF16)
        return carry

    def back(h, n):
        return lambda: over_x(3 + h, n, att_send.at[to_x(n), h], att.at[x, h]).start()

    for copy in own_qkv:
        copy.wait()
    for n in range(3):
        arrive_qkv(0, n)
    run(0, (0,))
    r0.step(1)
    r1.step(1)
    lax.fori_loop(0, 4, turn_updated, 0)
    for n in range(3):
        go(over_x(2, n, pair_send.at[to_x(n)], out_pair.at[:, block_of(x), :]))
    own_pair = pltpu.make_async_copy(pair_send.at[x], out_pair.at[:, block_of(x), :], own.at[5])
    own_pair.start()
    r2.step(1)
    r3.step(1)
    run(0, (1, -1))
    r0.step(2)
    r1.step(2)
    for n in range(3):
        arrive_qkv(1, n)
    run(1, (0, 1, -1))
    r2.step(2)
    r3.step(2)
    run(0, (2, -2))
    r0.step(3)
    r1.step(3)
    run(1, (2, -2))
    r2.step(3)
    r3.step(3)
    r0.finish()
    r1.finish()
    run(0, (3, -3, 4), (back(0, 2), back(0, 0), back(0, 1)))
    r2.finish()
    r3.finish()
    run(1, (3, -3, 4), (back(1, 2), back(1, 0), back(1, 1)))
    own_att = pltpu.make_async_copy(att_send.at[x], att.at[x], own.at[6])
    own_att.start()
    own_att.wait()
    for h in range(2):
        for n in (2, 0, 1):
            over_x(3 + h, n, att_send.at[0, h], att.at[from_x(n), h]).wait_recv()
        for k in range(NX):
            out_gated[2 * k + h] = (att[k, h].reshape(512, 128).astype(F32) * gate[k, h]).astype(BF16)

    own_pair.wait()
    for n in range(3):
        over_x(2, n, pair_send.at[0], out_pair.at[:, block_of(from_x(n)), :]).wait_recv()
    for h in range(2):
        for n in range(3):
            over_x(3 + h, n, att_send.at[to_x(n), h], att.at[x, h]).wait_send()
    for copy in sent:
        copy.wait_send()
    for one in (near, rest, r0, r1, r2, r3):
        one.drain()


def finish(gated, hom, pair, w_final, out_hom, out_pair):
    out_pair[...] = pair[...]
    quads = [regroup(*[gated[4 * b + t].astype(F32) for t in range(4)]) for b in range(2)]
    joined = jnp.concatenate(
        [jnp.concatenate([quads[0][s], quads[1][s]], axis=1).astype(BF16) for s in range(4)], axis=0
    )
    update = jnp.dot(joined, w_final[...], preferred_element_type=F32)
    out_hom[...] = (hom[...].astype(F32) + update.reshape(4, 128, 256)).astype(BF16)


def on_device(
    homolog_tensor,
    couple_tensor,
    homolog_presence,
    asking_matrix,
    lookup_matrix,
    content_matrix,
    sigmoid_matrix,
    sigmoid_offset,
    attention_final_matrix,
    first_factor_matrix,
    second_factor_matrix,
    tensor_product_matrix,
    couple_offset_matrix,
):
    vmem = pl.BlockSpec(memory_space=pltpu.VMEM)
    dma = pltpu.SemaphoreType.DMA
    scratch = [
        pltpu.VMEM((4, 512, 256), BF16),
        pltpu.VMEM((16, 32, 128), BF16),
        pltpu.VMEM((4, 16, 32, 128), BF16),
        pltpu.VMEM((4, 4, ROWS, 128), BF16),
        pltpu.VMEM((2, 4, 4, ROWS, 128), BF16),
        pltpu.VMEM((32 * ROWS, 128), F32),
        pltpu.VMEM((PLANES, 256, 128), BF16),
        pltpu.VMEM((2048, 128), F32),
        pltpu.VMEM((1024, 256), BF16),
        pltpu.VMEM((1024, 256), BF16),
        pltpu.VMEM((1024, 128), F32),
        pltpu.VMEM((128, 1024), BF16),
        pltpu.VMEM((4, 2, 2, 8, 4, 16, 128), BF16),
        pltpu.VMEM((4, 2, 2, 8, 4, 16, 128), BF16),
        pltpu.VMEM((4, 2, 128, 512), BF16),
        pltpu.VMEM((4, 2, 128, 512), BF16),
        pltpu.VMEM((4, 2, 512, 128), F32),
        pltpu.VMEM((4, 8, 128, 128), BF16),
        pltpu.VMEM((4, 8, 128, 128), F32),
        pltpu.VMEM((4, 8, 128, 128), BF16),
        pltpu.VMEM((32, 128), F32),
        pltpu.VMEM((32, 1024, 128), BF16),
        pltpu.VMEM((4, 8, 128, 128), BF16),
        pltpu.VMEM((8, 4, 8, 128), F32),
        pltpu.VMEM((2, 8, 4, 2, 8, 512), F32),
        pltpu.VMEM((128, 512), BF16),
        pltpu.VMEM((4, 2, 8, 4, 16, 128), BF16),
        pltpu.VMEM((4, 2, 8, 4, 16, 128), BF16),
        dma((11, 3)),
        dma((11, 3)),
        dma((5, 7)),
        dma((5, 7)),
        dma((15,)),
        dma((15,)),
        dma((6, 2, 4)),
        dma((6, 2, 4)),
        dma((9,)),
    ]
    gated, pair = pl.pallas_call(
        kernel,
        name="evoformer_block",
        out_shape=(
            jax.ShapeDtypeStruct((8, 512, 128), BF16),
            jax.ShapeDtypeStruct((8, 512, 128), BF16),
        ),
        in_specs=[vmem] * 12,
        out_specs=(vmem, vmem),
        scratch_shapes=scratch,
        compiler_params=pltpu.CompilerParams(
            collective_id=1, has_side_effects=True, vmem_limit_bytes=60 << 20
        ),
    )(
        homolog_tensor,
        couple_tensor,
        homolog_presence,
        asking_matrix,
        lookup_matrix,
        content_matrix,
        sigmoid_matrix,
        sigmoid_offset,
        first_factor_matrix.T,
        second_factor_matrix.T,
        tensor_product_matrix,
        couple_offset_matrix.T,
    )
    rows = lambda lead, width: pl.BlockSpec((lead, 128, width), lambda i: (0, i, 0))
    return pl.pallas_call(
        finish,
        name="final_projection",
        grid=(4,),
        out_shape=(
            jax.ShapeDtypeStruct((4, 512, 256), BF16),
            jax.ShapeDtypeStruct((8, 512, 128), BF16),
        ),
        in_specs=[
            rows(8, 128),
            rows(4, 256),
            rows(8, 128),
            pl.BlockSpec((256, 256), lambda i: (0, 0)),
        ],
        out_specs=(rows(4, 256), rows(8, 128)),
    )(gated, homolog_tensor, pair, attention_final_matrix)


def solution(mesh):
    return jax.shard_map(
        on_device,
        mesh=mesh,
        in_specs=(
            P(("dp", "dap"), None, None),
            P(("dp", "dap"), None, None),
            P(("dp", "dap"), None),
            P(),
            P(),
            P(),
            P(),
            P(),
            P(),
            P(),
            P(),
            P(),
            P(),
        ),
        out_specs=(P(("dp", "dap"), None, None), P(("dp", "dap"), None, None)),
        check_vma=False,
    )
```

```python
import functools
import math

import jax
import jax.numpy as jnp
from jax import lax
from jax.experimental import pallas as pl
from jax.experimental.pallas import tpu as pltpu
from jax.sharding import PartitionSpec as P

MESH = pl.DeviceIdType.MESH
F32 = jnp.float32
BF16 = jnp.bfloat16
LOG2E = math.log2(math.e)
SCORE_SCALE = 32.0**-0.5 * LOG2E
PENALTY = (56576.0, -7.46875, 0.01123046875)

NY, NX, NZ = 8, 4, 2
PLANES = 36
ROWS = 48
YZ_OFFSETS = [(dy, dz) for dz in range(NZ) for dy in range(NY) if (dy, dz) != (0, 0)]
X_OFFSETS = (1, 3, 2)
XZ_OFFSETS = [(dx, dz) for dx in (1, 3, 2, 0) for dz in range(NZ) if (dx, dz) != (0, 0)]


def wrap(value, size):
    return lax.rem(value + size, size)


def index_of(y, x, z):
    return (y * NX + x) * NZ + z


def remote(src, dst, send, recv, device):
    return pltpu.make_async_remote_copy(
        src_ref=src,
        dst_ref=dst,
        send_sem=send,
        recv_sem=recv,
        device_id={"dap": device},
        device_id_type=MESH,
    )


class Ring:
    def __init__(self, where, whole, half, send, recv):
        self.y, self.x, self.z = where
        self.whole, self.half = whole, half
        self.send, self.recv = send, recv

    def copy(self, way, step, block):
        view = self.half(block, way) if step == 3 else self.whole(block)
        to = wrap(self.y + (1 if way == 0 else -1), NY)
        return remote(
            view, view, self.send.at[way, step], self.recv.at[way, step], index_of(to, self.x, self.z)
        )

    def start(self):
        for way in (0, 1):
            self.copy(way, 0, self.y).start()

    def step(self, number):
        for way in (0, 1):
            block = wrap(self.y + (-number if way == 0 else number), NY)
            self.copy(way, number - 1, block).wait_recv()
            self.copy(way, number, block).start()

    def finish(self):
        for way in (0, 1):
            self.copy(way, 3, wrap(self.y + 4, NY)).wait_recv()

    def drain(self):
        for way in (0, 1):
            for step in range(4):
                self.copy(way, step, self.y).wait_send()


def regroup(v0, v1, v2, v3):
    lane = lax.broadcasted_iota(jnp.int32, v0.shape, 1)
    low = lane < 64
    even = lax.rem(lax.div(lane, 32), 2) == 0
    u0 = jnp.where(low, v0, pltpu.roll(v2, 64, 1))
    u2 = jnp.where(low, pltpu.roll(v0, 64, 1), v2)
    u1 = jnp.where(low, v1, pltpu.roll(v3, 64, 1))
    u3 = jnp.where(low, pltpu.roll(v1, 64, 1), v3)
    return (
        jnp.where(even, u0, pltpu.roll(u1, 32, 1)),
        jnp.where(even, pltpu.roll(u0, 96, 1), u1),
        jnp.where(even, u2, pltpu.roll(u3, 32, 1)),
        jnp.where(even, pltpu.roll(u2, 96, 1), u3),
    )


def perform(actions):
    for action in actions:
        action()


def normalize_rows(values):
    mean = jnp.mean(values, axis=-1, keepdims=True)
    centered = values - mean
    variance = jnp.mean(centered * centered, axis=-1, keepdims=True)
    return centered * lax.rsqrt(variance + 1e-05)


def nt_dot(left, right):
    return lax.dot_general(left, right, (((1,), (1,)), ((), ())), preferred_element_type=F32)


def kernel(
    hom,
    cpl,
    presence,
    w_query,
    w_key,
    w_value,
    w_gate,
    gate_offset,
    w_left_t,
    w_right_t,
    w_outer,
    w_bias_t,
    out_gated,
    out_pair,
    normed,
    l_send,
    l_all,
    r_send,
    r_got,
    r_wide,
    r_all,
    l_wide,
    l_mixed,
    l_t,
    w_outer_wide,
    w_outer_t,
    qv_send,
    qv,
    k_send,
    k_got,
    gate,
    couple,
    couple_t,
    updated_t,
    counts,
    outer,
    pair_send,
    bias_block,
    bias,
    penalty,
    att_send,
    att,
    x_send,
    x_recv,
    xz_send,
    xz_recv,
    yz_send,
    yz_recv,
    ring_send,
    ring_recv,
    att_out,
    att_in,
    own,
):
    me = lax.axis_index("dap")
    y = lax.div(me, NX * NZ)
    x = lax.rem(lax.div(me, NZ), NX)
    z = lax.rem(me, NZ)
    yz = y * NZ + z
    where = (y, x, z)

    barrier = pltpu.get_barrier_semaphore()
    for dx, dz in XZ_OFFSETS:
        if dx != 0:
            pl.semaphore_signal(
                barrier,
                inc=1,
                device_id={"dap": index_of(y, wrap(x + dx, NX), wrap(z + dz, NZ))},
                device_id_type=MESH,
            )
    for dy, dz in YZ_OFFSETS:
        pl.semaphore_signal(
            barrier,
            inc=1,
            device_id={"dap": index_of(wrap(y + dy, NY), x, wrap(z + dz, NZ))},
            device_id_type=MESH,
        )

    def over_x(kind, n, src, dst):
        to = index_of(y, wrap(x + X_OFFSETS[n], NX), z)
        return remote(src, dst, x_send.at[kind, n], x_recv.at[kind, n], to)

    def over_xz(kind, n, src, dst):
        dx, dz = XZ_OFFSETS[n]
        to = index_of(y, wrap(x + dx, NX), wrap(z + dz, NZ))
        return remote(src, dst, xz_send.at[kind, n], xz_recv.at[kind, n], to)

    def to_xz(n):
        return wrap(x + XZ_OFFSETS[n][0], NX)

    def from_xz(n):
        dx, dz = XZ_OFFSETS[n]
        return wrap(x - dx, NX), wrap(z - dz, NZ)

    def to_x(n):
        return wrap(x + X_OFFSETS[n], NX)

    def from_x(n):
        return wrap(x - X_OFFSETS[n], NX)

    sent = []

    def go(copy):
        copy.start()
        sent.append(copy)

    def block_of(k):
        return pl.ds(pl.multiple_of(128 * k, 128), 128)

    lanes = lax.broadcasted_iota(jnp.int32, (512, 128), 1)
    groups = lax.div(lanes, 32)

    def project_right(s, carry):
        lines = normalize_rows(hom[s].astype(F32)).astype(BF16)
        normed[s] = lines
        present = presence[pl.ds(s, 1), :].astype(F32)
        right = (nt_dot(w_right_t[...], lines) * present).astype(BF16)
        rows = jnp.concatenate(
            [present[:, 128 * k : 128 * k + 128] for k in range(4)] + [jnp.zeros((12, 128), F32)], axis=0
        ).astype(BF16)
        for k in range(NX):
            r_send[k, s, 0:32, :] = right[:, 128 * k : 128 * k + 128]
            r_send[k, s, 32:48, :] = rows
        return carry

    lax.fori_loop(0, 4, project_right, 0)
    pl.semaphore_wait(barrier, 6 + len(YZ_OFFSETS))
    for n in range(7):
        go(over_xz(0, n, r_send.at[to_xz(n)], r_got.at[z, x]))

    w_left = jnp.concatenate([w_left_t[...]] * 4, axis=0)

    def project_left(s, total):
        return jnp.where(groups == s, nt_dot(normed[s], w_left), total)

    left = lax.fori_loop(0, 4, project_left, jnp.zeros((512, 128), F32))
    spread = jnp.where(
        lax.div(lax.broadcasted_iota(jnp.int32, (128, 128), 1), 32)
        == lax.broadcasted_iota(jnp.int32, (128, 128), 0),
        1.0,
        0.0,
    ).astype(BF16)
    tall = jnp.concatenate([presence[...].astype(F32), jnp.zeros((124, 512), F32)], axis=0).T
    left = left * jnp.dot(tall.astype(BF16), spread, preferred_element_type=F32)
    left = left.reshape(NY, NX, NZ, 8, 128)
    for b in range(NY):
        for c in range(NZ):
            l_send[b * NZ + c] = left[b, :, c].reshape(32, 128).astype(BF16)

    for n, (dy, dz) in enumerate(YZ_OFFSETS):
        to_y, to_z = wrap(y + dy, NY), wrap(z + dz, NZ)
        go(
            remote(
                l_send.at[to_y * NZ + to_z],
                l_all.at[x, yz],
                yz_send.at[n],
                yz_recv.at[n],
                index_of(to_y, x, to_z),
            )
        )
    for n in range(3):
        go(over_x(1, n, cpl.at[:, block_of(to_x(n)), :], couple.at[x]))
    own_copies = [
        pltpu.make_async_copy(r_send.at[x], r_got.at[z, x], own.at[0]),
        pltpu.make_async_copy(l_send.at[yz], l_all.at[x, yz], own.at[1]),
        pltpu.make_async_copy(cpl.at[:, block_of(x), :], couple.at[x], own.at[2]),
    ]
    for copy in own_copies:
        copy.start()

    def heads(part, carry):
        rows = pl.ds(pl.multiple_of(128 * part, 128), 128)
        for kind, w in enumerate((w_query, w_value, w_gate)):
            made = [jnp.dot(normed[s, rows, :], w[...], preferred_element_type=F32) for s in range(4)]
            if kind == 2:
                made = [jax.nn.sigmoid(m + offset_row) for m in made]
            for b in range(2):
                outs = regroup(*[m[:, 128 * b : 128 * b + 128] for m in made])
                for t in range(4):
                    h = 4 * b + t
                    if kind == 2:
                        gate[h // 2, h % 2, rows, :] = outs[t]
                    else:
                        qv_send[h // 2, h % 2, kind, pl.ds(2 * part, 2)] = (
                            outs[t].astype(BF16).reshape(2, 4, 16, 128)
                        )
        return carry

    offset_row = gate_offset[...].astype(F32).reshape(1, 256)
    w_key_t = w_key[...].astype(F32).T.astype(BF16)

    def keys(s, carry):
        made = nt_dot(w_key_t, normed[s]).astype(BF16)
        for h in range(8):
            k_send[h // 2, h % 2, pl.ds(pl.multiple_of(32 * s, 32), 32), :] = made[32 * h : 32 * h + 32]
        return carry

    lax.fori_loop(0, 4, keys, 0)
    lax.fori_loop(0, 4, heads, 0)

    def qkv_copies(h, n):
        other = from_x(n)
        return (
            (5 + 3 * h, k_send.at[to_x(n), h], k_got.at[x, h], k_got.at[other, h]),
            (6 + 3 * h, qv_send.at[to_x(n), h, 1], qv.at[x, h, 1], qv.at[other, h, 1]),
            (7 + 3 * h, qv_send.at[to_x(n), h, 0], qv.at[x, h, 0], qv.at[other, h, 0]),
        )

    def send_qkv(h, kinds=(0, 1, 2)):
        for k in kinds:
            for n in range(3):
                kind, src, dst, _ = qkv_copies(h, n)[k]
                go(over_x(kind, n, src, dst))

    def arrive_qkv(h, n):
        for kind, src, _, got in qkv_copies(h, n):
            over_x(kind, n, src, got).wait_recv()

    own_qkv = [
        pltpu.make_async_copy(k_send.at[x], k_got.at[x], own.at[3]),
        pltpu.make_async_copy(qv_send.at[x], qv.at[x], own.at[7]),
    ]
    for copy in own_qkv:
        copy.start()

    own_copies[0].wait()
    for n in range(7):
        other_x, other_z = from_xz(n)
        over_xz(0, n, r_send.at[0], r_got.at[other_z, other_x]).wait_recv()
    r_wide[...] = r_got[...].astype(F32).reshape(32 * ROWS, 128)

    def line_of(b):
        return pl.ds(pl.multiple_of(32 * b, 32), 32)

    for q in range(PLANES):
        r_all[q, line_of(y), :] = r_wide[pl.ds(q, 32, stride=ROWS), :].astype(BF16)

    def right_ring(c):
        first = (0, 18)[c]

        def whole(b):
            return r_all.at[pl.ds(first, 18), line_of(b), :]

        def half(b, way):
            return r_all.at[pl.ds(first + 9 * way, 9), line_of(b), :]

        return Ring(where, whole, half, ring_send.at[c], ring_recv.at[c])

    near, rest = right_ring(0), right_ring(1)
    near.start()
    rest.start()

    own_copies[1].wait()
    for n, (dy, dz) in enumerate(YZ_OFFSETS):
        from_yz = wrap(y - dy, NY) * NZ + wrap(z - dz, NZ)
        remote(l_send.at[0], l_all.at[x, from_yz], yz_send.at[n], yz_recv.at[n], me).wait_recv()
    for n in range(3):
        go(over_x(0, n, l_all.at[x], l_all.at[x]))
    send_qkv(0)

    near.step(1)
    rest.step(1)

    w_outer_wide[...] = w_outer[...].astype(F32)
    for k in range(8):
        w_outer_t[:, 128 * k : 128 * k + 128] = (
            jnp.concatenate([w_outer_wide[pl.ds(4 * k + t, 32, stride=32), :] for t in range(4)], axis=0)
            .T.astype(BF16)
        )

    near.step(2)
    rest.step(2)

    for n in range(3):
        over_x(0, n, l_all.at[x], l_all.at[from_x(n)]).wait_recv()
    l_wide[...] = l_all[...].astype(F32).reshape(2048, 128)
    for pair in range(16):
        block = jnp.concatenate(
            [l_wide[pl.ds(2 * pair, 64, stride=32), :], l_wide[pl.ds(2 * pair + 1, 64, stride=32), :]],
            axis=0,
        ).T
        for e in range(2):
            l_mixed[pl.ds((2 * pair + e) * 32, 32), :] = jnp.concatenate(
                [block[32 * s : 32 * s + 32, 64 * e : 64 * e + 64] for s in range(4)], axis=1
            ).astype(BF16)
    source = lax.broadcasted_iota(jnp.int32, (256, 256), 0)
    target = lax.broadcasted_iota(jnp.int32, (256, 256), 1)
    place = lax.rem(source, 16) * 16 + lax.rem(lax.div(source, 16), 4) * 4 + lax.div(source, 64)
    order = jnp.where(place == target, 1.0, 0.0).astype(BF16)
    l_t[...] = jnp.dot(l_mixed[...], order, preferred_element_type=F32).astype(BF16)

    own_copies[2].wait()
    for n in range(3):
        over_x(1, n, cpl.at[:, pl.ds(0, 128), :], couple.at[from_x(n)]).wait_recv()

    def turn_couple(g, carry):
        for i in range(8):
            couple_t[g, i] = couple[g, i].astype(F32).T
        return carry

    lax.fori_loop(0, 4, turn_couple, 0)
    near.step(3)
    send_qkv(1, (0, 1))
    rest.step(3)
    near.finish()

    def outer_rows(g, first, last):
        l_rows = l_t[pl.ds(pl.multiple_of(g * 256, 256), 256), :]
        for d in range(first, last):
            right = jnp.concatenate([r_all[2 * d], r_all[2 * d + 1]], axis=1)
            product = jnp.dot(l_rows, right, preferred_element_type=F32).astype(BF16)
            for e in range(2):
                outer[pl.ds(8 * g, 8), (2 * d + e) * 32 : (2 * d + e) * 32 + 32, :] = product[
                    :, 128 * e : 128 * e + 128
                ].reshape(8, 32, 128)

    def outer_near(g, carry):
        outer_rows(g, 0, 9)
        return carry

    lax.fori_loop(0, 4, outer_near, 0)
    rest.finish()

    plane = r_all[32 + lax.div(y, 2)].astype(F32).T.astype(BF16)
    together = jnp.dot(plane, r_all[32 + x], preferred_element_type=F32).astype(BF16)
    row = lax.broadcasted_iota(jnp.int32, (32, 128), 0)
    column = lax.broadcasted_iota(jnp.int32, (32, 128), 1)
    chosen = 64 * lax.rem(y, 2) + 16 * lax.div(row, 8) + 8 * z + lax.rem(row, 8)
    pick = jnp.where(chosen == column, 1.0, 0.0).astype(BF16)
    counts[...] = 1.0 / (jnp.dot(pick, together, preferred_element_type=F32) + 0.001)

    w_bias = jnp.concatenate([w_bias_t[...]] * 3, axis=1)

    def outer_rest(g, carry):
        outer_rows(g, 9, 16)
        offsets = []
        for pair in range(4):
            right = jnp.concatenate([outer[8 * g + 2 * pair], outer[8 * g + 2 * pair + 1]], axis=1)
            update = jnp.dot(w_outer_t[...], right, preferred_element_type=F32)
            standards = []
            for e in range(2):
                i = 2 * pair + e
                scaled = update[:, 128 * e : 128 * e + 128] * counts[pl.ds(g * 8 + i, 1), :]
                updated = (couple_t[g, i] + scaled).astype(BF16)
                updated_t[g, i] = updated
                updated = updated.astype(F32)
                mean = jnp.mean(updated, axis=0, keepdims=True)
                centered = updated - mean
                variance = jnp.mean(centered * centered, axis=0, keepdims=True)
                standards.append(centered * lax.rsqrt(variance + 1e-05))
            standard = jnp.concatenate(standards, axis=1)
            part_a = standard.astype(BF16)
            left_over = standard - part_a.astype(F32)
            part_b = left_over.astype(BF16)
            part_c = (left_over - part_b.astype(F32)).astype(BF16)
            both = (
                jnp.dot(
                    w_bias, jnp.concatenate([part_a, part_b, part_c], axis=0), preferred_element_type=F32
                )
                * LOG2E
            )
            offsets += [both[:, :128], both[:, 128:]]
        for h in range(8):
            bias_block[h, g] = jnp.concatenate([v[h : h + 1] for v in offsets], axis=0)
        return carry

    def send_bias(c):
        half_rows = pl.ds(2 * c, 2)
        for h in range(2):
            for n in range(7):
                go(
                    over_xz(
                        1 + 2 * c + h,
                        n,
                        bias_block.at[2 * to_xz(n) + h, half_rows],
                        bias.at[h, y, half_rows, z, :, block_of(x)],
                    )
                )
        copy = pltpu.make_async_copy(
            bias_block.at[pl.ds(2 * x, 2), half_rows],
            bias.at[:, y, half_rows, z, :, block_of(x)],
            own.at[(4, 8)[c]],
        )
        copy.start()
        return copy

    lax.fori_loop(0, 2, outer_rest, 0)
    own_bias = [send_bias(0)]
    lax.fori_loop(2, 4, outer_rest, 0)
    own_bias.append(send_bias(1))

    present = jnp.concatenate([r_all[32 + k, pl.ds(pl.multiple_of(16 * yz, 16), 16), :] for k in range(4)], axis=1).astype(F32) - 1.0
    penalty[...] = jnp.concatenate(
        [present * PENALTY[0], present * PENALTY[1], present * PENALTY[2], jnp.zeros((80, 512), F32)],
        axis=0,
    ).astype(BF16)

    def arrive_bias(c):
        half_rows = pl.ds(2 * c, 2)
        own_bias[c].wait()
        for h in range(2):
            for n in range(7):
                other_x, other_z = from_xz(n)
                over_xz(
                    1 + 2 * c + h,
                    n,
                    bias_block.at[0, half_rows],
                    bias.at[h, y, half_rows, other_z, :, block_of(other_x)],
                ).wait_recv()

    def bias_ring(h, c):
        def whole(b):
            return bias.at[h, b, pl.ds(2 * c, 2)]

        def half(b, way):
            return bias.at[h, b, 2 * c + way]

        number = 2 + 2 * h + c
        return Ring(where, whole, half, ring_send.at[number], ring_recv.at[number])

    r0, r1, r2, r3 = [bias_ring(h, c) for h in range(2) for c in range(2)]
    arrive_bias(0)
    r0.start()
    r2.start()
    arrive_bias(1)
    r1.start()
    r3.start()
    send_qkv(1, (2,))

    def attend(h, owner, blocks):
        count = 64 * len(blocks)
        lane = lax.broadcasted_iota(jnp.int32, (count, 128), 1)
        offset = jnp.concatenate([bias[h, b].reshape(64, 512) for b in blocks], axis=0)
        query = jnp.concatenate([qv[owner, h, 0, b].reshape(64, 128) for b in blocks], axis=0)
        every = qv[owner, h, 1].reshape(512, 128)
        weights, values = [], []
        for e in range(4):
            inside = groups == e
            keys = [jnp.zeros((32, 512), BF16)] * 4
            keys[e] = k_got[owner, h, 32 * e : 32 * e + 32, :]
            key = jnp.concatenate(keys + [penalty[...]], axis=0)
            value = jnp.where(inside, every, jnp.zeros((), BF16))
            values.append(jnp.concatenate([value, jnp.where(inside, 1.0, 0.0).astype(BF16)], axis=1))
            marked = (lax.rem(lane, 16) == owner * 4 + e) & (lane < 48)
            left = jnp.concatenate([query, jnp.where(marked, 1.0, 0.0).astype(BF16)], axis=1)
            scores = jnp.dot(left, key, preferred_element_type=F32) * SCORE_SCALE + offset
            top = jnp.max(scores, axis=-1, keepdims=True)
            weights.append(jnp.exp2(scores - top).astype(BF16))
        both = jnp.dot(
            jnp.concatenate(weights, axis=1),
            jnp.concatenate(values, axis=0),
            preferred_element_type=F32,
        )
        result = (both[:, :128] / both[:, 128:]).astype(BF16).reshape(len(blocks), 4, 16, 128)
        for k, b in enumerate(blocks):
            att_send[owner, h, b] = result[k]

    def back(h, n, o):
        b = wrap(y + o, NY)
        return remote(
            att_send.at[to_x(n), h, b],
            att.at[x, h, b],
            att_out.at[h, n, o % NY],
            att_in.at[h, n, o % NY],
            index_of(y, to_x(n), z),
        )

    def run(h, offsets):
        blocks = [wrap(y + o, NY) for o in offsets]

        def body(k, carry):
            shift = jnp.where(k == 0, 2, jnp.where(k == 1, 1, jnp.where(k == 2, 3, 0)))
            attend(h, wrap(x + shift, NX), blocks)
            for slot, n in enumerate((2, 0, 1)):
                pl.when(k == slot)(lambda n=n: perform([back(h, n, o).start for o in offsets]))
            return carry

        lax.fori_loop(0, 4, body, 0)

    def turn_updated(g, carry):
        for i in range(8):
            pair_send[g, i] = updated_t[g, i].astype(F32).T.astype(BF16)
        return carry

    for copy in own_qkv:
        copy.wait()
    for n in range(3):
        arrive_qkv(0, n)
    run(0, (0,))
    r0.step(1)
    r1.step(1)
    lax.fori_loop(0, 4, turn_updated, 0)
    for n in range(3):
        go(over_x(2, n, pair_send.at[to_x(n)], out_pair.at[:, block_of(x), :]))
    own_pair = pltpu.make_async_copy(pair_send.at[x], out_pair.at[:, block_of(x), :], own.at[5])
    own_pair.start()
    r2.step(1)
    r3.step(1)
    run(0, (1, -1))
    r0.step(2)
    r1.step(2)
    for n in range(3):
        arrive_qkv(1, n)
    run(1, (0, 1, -1))
    r2.step(2)
    r3.step(2)
    run(0, (2, -2))
    r0.step(3)
    r1.step(3)
    run(1, (2, -2))
    r2.step(3)
    r3.step(3)
    r0.finish()
    r1.finish()
    run(0, (3, -3, 4))
    r2.finish()
    r3.finish()
    run(1, (3, -3, 4))
    own_att = pltpu.make_async_copy(att_send.at[x], att.at[x], own.at[6])
    own_att.start()
    own_att.wait()
    for h in range(2):
        for n in (2, 0, 1):
            for o in range(NY):
                b = wrap(y + o, NY)
                remote(
                    att_send.at[0, h, b], att.at[from_x(n), h, b], att_out.at[h, n, o], att_in.at[h, n, o], me
                ).wait_recv()
        for k in range(NX):
            out_gated[2 * k + h] = (att[k, h].reshape(512, 128).astype(F32) * gate[k, h]).astype(BF16)

    own_pair.wait()
    for n in range(3):
        over_x(2, n, pair_send.at[0], out_pair.at[:, block_of(from_x(n)), :]).wait_recv()
    for h in range(2):
        for n in range(3):
            for o in range(NY):
                back(h, n, o).wait_send()
    for copy in sent:
        copy.wait_send()
    for one in (near, rest, r0, r1, r2, r3):
        one.drain()


def finish(gated, hom, pair, w_final, out_hom, out_pair):
    out_pair[...] = pair[...]
    quads = [regroup(*[gated[4 * b + t].astype(F32) for t in range(4)]) for b in range(2)]
    joined = jnp.concatenate(
        [jnp.concatenate([quads[0][s], quads[1][s]], axis=1).astype(BF16) for s in range(4)], axis=0
    )
    update = jnp.dot(joined, w_final[...], preferred_element_type=F32)
    out_hom[...] = (hom[...].astype(F32) + update.reshape(4, 128, 256)).astype(BF16)


def on_device(
    homolog_tensor,
    couple_tensor,
    homolog_presence,
    asking_matrix,
    lookup_matrix,
    content_matrix,
    sigmoid_matrix,
    sigmoid_offset,
    attention_final_matrix,
    first_factor_matrix,
    second_factor_matrix,
    tensor_product_matrix,
    couple_offset_matrix,
):
    vmem = pl.BlockSpec(memory_space=pltpu.VMEM)
    dma = pltpu.SemaphoreType.DMA
    scratch = [
        pltpu.VMEM((4, 512, 256), BF16),
        pltpu.VMEM((16, 32, 128), BF16),
        pltpu.VMEM((4, 16, 32, 128), BF16),
        pltpu.VMEM((4, 4, ROWS, 128), BF16),
        pltpu.VMEM((2, 4, 4, ROWS, 128), BF16),
        pltpu.VMEM((32 * ROWS, 128), F32),
        pltpu.VMEM((PLANES, 256, 128), BF16),
        pltpu.VMEM((2048, 128), F32),
        pltpu.VMEM((1024, 256), BF16),
        pltpu.VMEM((1024, 256), BF16),
        pltpu.VMEM((1024, 128), F32),
        pltpu.VMEM((128, 1024), BF16),
        pltpu.VMEM((4, 2, 2, 8, 4, 16, 128), BF16),
        pltpu.VMEM((4, 2, 2, 8, 4, 16, 128), BF16),
        pltpu.VMEM((4, 2, 128, 512), BF16),
        pltpu.VMEM((4, 2, 128, 512), BF16),
        pltpu.VMEM((4, 2, 512, 128), F32),
        pltpu.VMEM((4, 8, 128, 128), BF16),
        pltpu.VMEM((4, 8, 128, 128), F32),
        pltpu.VMEM((4, 8, 128, 128), BF16),
        pltpu.VMEM((32, 128), F32),
        pltpu.VMEM((32, 1024, 128), BF16),
        pltpu.VMEM((4, 8, 128, 128), BF16),
        pltpu.VMEM((8, 4, 8, 128), F32),
        pltpu.VMEM((2, 8, 4, 2, 8, 512), F32),
        pltpu.VMEM((128, 512), BF16),
        pltpu.VMEM((4, 2, 8, 4, 16, 128), BF16),
        pltpu.VMEM((4, 2, 8, 4, 16, 128), BF16),
        dma((11, 3)),
        dma((11, 3)),
        dma((5, 7)),
        dma((5, 7)),
        dma((15,)),
        dma((15,)),
        dma((6, 2, 4)),
        dma((6, 2, 4)),
        dma((2, 3, 8)),
        dma((2, 3, 8)),
        dma((9,)),
    ]
    gated, pair = pl.pallas_call(
        kernel,
        name="evoformer_block",
        out_shape=(
            jax.ShapeDtypeStruct((8, 512, 128), BF16),
            jax.ShapeDtypeStruct((8, 512, 128), BF16),
        ),
        in_specs=[vmem] * 12,
        out_specs=(vmem, vmem),
        scratch_shapes=scratch,
        compiler_params=pltpu.CompilerParams(
            collective_id=1, has_side_effects=True, vmem_limit_bytes=60 << 20
        ),
    )(
        homolog_tensor,
        couple_tensor,
        homolog_presence,
        asking_matrix,
        lookup_matrix,
        content_matrix,
        sigmoid_matrix,
        sigmoid_offset,
        first_factor_matrix.T,
        second_factor_matrix.T,
        tensor_product_matrix,
        couple_offset_matrix.T,
    )
    rows = lambda lead, width: pl.BlockSpec((lead, 128, width), lambda i: (0, i, 0))
    return pl.pallas_call(
        finish,
        name="final_projection",
        grid=(4,),
        out_shape=(
            jax.ShapeDtypeStruct((4, 512, 256), BF16),
            jax.ShapeDtypeStruct((8, 512, 128), BF16),
        ),
        in_specs=[
            rows(8, 128),
            rows(4, 256),
            rows(8, 128),
            pl.BlockSpec((256, 256), lambda i: (0, 0)),
        ],
        out_specs=(rows(4, 256), rows(8, 128)),
    )(gated, homolog_tensor, pair, attention_final_matrix)


def solution(mesh):
    return jax.shard_map(
        on_device,
        mesh=mesh,
        in_specs=(
            P(("dp", "dap"), None, None),
            P(("dp", "dap"), None, None),
            P(("dp", "dap"), None),
            P(),
            P(),
            P(),
            P(),
            P(),
            P(),
            P(),
            P(),
            P(),
            P(),
        ),
        out_specs=(P(("dp", "dap"), None, None), P(("dp", "dap"), None, None)),
        check_vma=False,
    )
```
